256 devices in a mesh: dp: 16 (over x, y), expert: 16 (over z, core).
Axes of the slice: x: 4, y: 4, z: 8, core: 2. Of those that a mesh axis runs over, the one named last changes fastest.
Arguments:
- tokens: bfloat16 [32768, 1440], P(('dp', 'expert')), parts along dimension 0, may hold values from -6 to 6
- route_ids: int32 [32768, 4], P(('dp', 'expert')), parts along dimension 0, may hold values from 0 to 15, as said below
- route_level: int32 [32768, 4], P(('dp', 'expert')), parts along dimension 0, may hold values from 0 to 15
- gate_up_codes: int32 [16, 1440, 720], P('expert'), may hold values from 0 to 65535
- gate_up_scale: int32 [16, 45, 2880], P('expert'), may hold values from 119 to 122
- gate_up_bias: bfloat16 [16, 2880], P('expert'), may hold values from -3 to 3
- down_codes: int32 [16, 1440, 360], P('expert'), may hold values from 0 to 65535
- down_scale: int32 [16, 45, 1440], P('expert'), may hold values from 117 to 120
- down_bias: bfloat16 [16, 1440], P('expert'), may hold values from -3 to 3
- attn_gain: bfloat16 [1440], replicated, may hold values from 0.5 to 1.5
- query_weight: bfloat16 [1440, 2048], replicated, may hold values from -14 to 14
- key_matrix: bfloat16 [1440, 256], replicated, may hold values from -1 to 1
- value_matrix: bfloat16 [1440, 256], replicated, may hold values from -0.15625 to 0.15625
- sinks: float32 [32], replicated, may hold values from 4 to 12
Outputs:
- block_out: bfloat16 [32768, 1440], P(('dp', 'expert')), parts along dimension 0
- attended: bfloat16 [32768, 2048], P(('dp', 'expert')), parts along dimension 0
The draws below stay inside these ranges and needn't reach their ends.
There are 16 independent parts, one for each index of `dp`. The reference program is written for one: setup_inputs(seed, part) draws one part's arguments, and reference() takes and returns one part's arrays. A program takes and returns all parts, laid end to end along the dimension named above; an argument that names none is the same for every part. Nothing has to cross between parts.
Inputs may be any that keep to these rules, and one draw needn't show every extreme that they name: `route_ids`: each row names 4 different experts. Among the 128 rows of one device no expert is named more than 64 times, and one expert is named exactly 64 times on each.
All inputs are finite; a program needn't handle non-finite values.
Results may differ from the reference program's by a relative error of at most 0.015.
The reference program's roundings to bfloat16 on the way count: a program that leaves them out, or rounds other values in their place, can miss the bound.
Values may be sent and summed in bfloat16 or wider, within the bound.
No kernel may reach another device: no remote copies, remote signals or barrier semaphores. Data moves between devices by JAX's collectives and lax.ppermute only.
A program may use at most 128 MiB of HBM per device.

```python
import math
import jax
import jax.numpy as jnp
from jax import lax

MODEL_FEATURES = 1440
FF = 1440
TOPK = 4
QUERY_HEAD_COUNT = 32
KEY_VALUE_HEADS = 4
HEAD_SIZE = 64
WINDOW_LENGTH = 128
TOK_DEV = 128
EXPERTS = 16
TOKEN_COUNT = 2048
MOST = 64


def draw_route_ids(key, part):
    key = jax.random.fold_in(key, 11)
    hot_expert = jax.random.randint(jax.random.fold_in(key, 1), (), 0, EXPERTS).astype(jnp.int32)
    block_count = TOKEN_COUNT // TOK_DEV
    slot_count = TOK_DEV * TOPK
    seat_count = (EXPERTS - 1) * MOST

    def one_block(block_index):
        block_key = jax.random.fold_in(key, block_index + 2)
        chosen = jax.random.permutation(jax.random.fold_in(block_key, 0), seat_count)[:slot_count - MOST].astype(jnp.int32)
        others = chosen // MOST
        others = others + (others >= hot_expert).astype(jnp.int32)
        expert_ids = jnp.sort(jnp.concatenate([jnp.full((MOST,), hot_expert, jnp.int32), others]))
        table = expert_ids.reshape(TOPK, TOK_DEV).T
        rolled = jax.random.randint(jax.random.fold_in(block_key, 2), (TOK_DEV,), 0, TOPK)
        columns = (jnp.arange(TOPK, dtype=jnp.int32)[None, :] + rolled[:, None]) % TOPK
        table = jnp.take_along_axis(table, columns, axis=1)
        row_order = jax.random.permutation(jax.random.fold_in(block_key, 1), TOK_DEV)
        return table[row_order]
    return jax.vmap(one_block)(jnp.arange(block_count)).reshape(TOKEN_COUNT, TOPK).astype(jnp.int32)


def shared_keys(key):
    key = jax.random.fold_in(key, 21)
    scattered_rows = 2.0 / math.sqrt(MODEL_FEATURES)
    return jnp.clip(jax.random.normal(key, (MODEL_FEATURES, KEY_VALUE_HEADS * HEAD_SIZE), jnp.float32), -4.0, 4.0) * scattered_rows


def draw_key_matrix(key, part):
    return shared_keys(key).astype(jnp.bfloat16)


def draw_query_weight(key, part):
    key = jax.random.fold_in(key, 22)
    scattered_rows = 2.0 / math.sqrt(MODEL_FEATURES)
    result = jnp.clip(jax.random.normal(jax.random.fold_in(key, 0), (MODEL_FEATURES, QUERY_HEAD_COUNT * HEAD_SIZE), jnp.float32), -4.0, 4.0) * scattered_rows
    return result.astype(jnp.bfloat16)


def set_ends(array, own_key, low, largest):
    extent = array.shape
    index_at = [jax.random.randint(jax.random.fold_in(own_key, axis), (), 0, extent[axis]) for axis in range(len(extent))]
    array = array.at[tuple(index_at)].set(low)
    longest = extent.index(max(extent))
    index_at[longest] = (index_at[longest] + 1) % extent[longest]
    return array.at[tuple(index_at)].set(largest)


def steps_of(stream_key, dims, cuts, least, top_value):
    def one(dim, parts):
        steps = jax.random.uniform(jax.random.fold_in(jax.random.fold_in(stream_key, 6), dim), (parts,), jnp.float32, least / len(cuts), top_value / len(cuts))
        return jnp.repeat(jnp.exp(steps), dims[dim] // parts).reshape((-1,) + (1,) * (len(dims) - dim - 1))

    loudness = one(*cuts[0])
    for cut in cuts[1:]:
        loudness = loudness * one(*cut)
    return loudness


def bell_draw(rng, dims, deviation, most, cuts=(), kind=jnp.bfloat16):
    entries = deviation * jax.random.normal(rng, dims, jnp.float32)
    if cuts:
        entries = entries * steps_of(rng, dims, cuts, -0.22, 0.18)
    return jnp.clip(entries, -most, most).astype(kind)


def setup_inputs(seed: int = 0, part: int = 0) -> dict:
    streams_of = jax.random.split(jax.random.key(seed), 15)
    part_keys = jax.random.split(jax.random.fold_in(streams_of[14], part), 15)
    tokens = bell_draw(part_keys[0], (TOKEN_COUNT, MODEL_FEATURES), 1.0, 6.0, ((0, 16),))
    route_ids = draw_route_ids(jax.random.fold_in(jax.random.fold_in(streams_of[14], part), 71), part)
    route_level = set_ends(jax.random.randint(part_keys[2], (TOKEN_COUNT, TOPK), 0, 16), jax.random.fold_in(part_keys[2], 1), 0, 15).astype(jnp.int32)
    gate_up_codes = set_ends(jax.random.randint(streams_of[3], (EXPERTS, MODEL_FEATURES, FF // 2), 0, 65536), jax.random.fold_in(streams_of[3], 1), 0, 65535).astype(jnp.int32)
    gate_up_scale = set_ends(jax.random.randint(streams_of[4], (EXPERTS, MODEL_FEATURES // 32, 2 * FF), 119, 123), jax.random.fold_in(streams_of[4], 1), 119, 122).astype(jnp.int32)
    gate_up_bias = bell_draw(streams_of[5], (EXPERTS, 2 * FF), 0.5, 3.0, ((0, 16),))
    down_codes = set_ends(jax.random.randint(streams_of[6], (EXPERTS, FF, MODEL_FEATURES // 4), 0, 65536), jax.random.fold_in(streams_of[6], 1), 0, 65535).astype(jnp.int32)
    down_scale = set_ends(jax.random.randint(streams_of[7], (EXPERTS, FF // 32, MODEL_FEATURES), 117, 121), jax.random.fold_in(streams_of[7], 1), 117, 120).astype(jnp.int32)
    down_bias = bell_draw(streams_of[8], (EXPERTS, MODEL_FEATURES), 0.5, 3.0, ((0, 16),))
    attn_gain = jnp.clip(1.0 + 0.1 * jax.random.normal(streams_of[9], (MODEL_FEATURES,), jnp.float32), 0.5, 1.5).astype(jnp.bfloat16)
    query_weight = draw_query_weight(jax.random.fold_in(streams_of[14], 71), part)
    key_matrix = draw_key_matrix(jax.random.fold_in(streams_of[14], 71), part)
    value_matrix = bell_draw(streams_of[12], (MODEL_FEATURES, KEY_VALUE_HEADS * HEAD_SIZE), MODEL_FEATURES ** -0.5, 0.15625)
    sinks = jnp.clip(jax.random.uniform(streams_of[13], (QUERY_HEAD_COUNT,), jnp.float32, 4.0, 12.0), 4.0, 12.0)
    return dict(tokens=tokens, route_ids=route_ids, route_level=route_level, gate_up_codes=gate_up_codes, gate_up_scale=gate_up_scale, gate_up_bias=gate_up_bias, down_codes=down_codes, down_scale=down_scale, down_bias=down_bias, attn_gain=attn_gain, query_weight=query_weight, key_matrix=key_matrix, value_matrix=value_matrix, sinks=sinks)


def decode_weights(packed_words, exponents):
    shift_bits = 4 * jnp.arange(4, dtype=jnp.int32)
    nibbles = jnp.bitwise_and(jnp.right_shift(packed_words[..., None], shift_bits), 15)
    nibbles = nibbles.reshape(packed_words.shape[:-1] + (packed_words.shape[-1] * 4,))
    low_bits = jnp.bitwise_and(nibbles, 7)
    exponent_bits = jnp.right_shift(low_bits, 1)
    mantissa = jnp.bitwise_and(low_bits, 1).astype(jnp.float32)
    normal_part = jnp.exp2((exponent_bits - 1).astype(jnp.float32)) * (1.0 + 0.5 * mantissa)
    magnitude = jnp.where(exponent_bits == 0, 0.5 * mantissa, normal_part)
    signed_value = jnp.where(nibbles >= 8, -magnitude, magnitude)
    block_scale = jnp.repeat(jnp.exp2((exponents - 127).astype(jnp.float32)), 32, axis=packed_words.ndim - 2)
    return (signed_value * block_scale).astype(jnp.bfloat16)

def expert_rows(selected_rows, first_weight, second_weight, first_bias, second_bias):
    pre_act = jnp.dot(selected_rows, first_weight, preferred_element_type=jnp.float32) + first_bias.astype(jnp.float32)
    gate_part = jnp.minimum(pre_act[:, 0::2], 7.0)
    up_part = jnp.clip(pre_act[:, 1::2], -7.0, 7.0)
    activated = ((up_part + 1.0) * gate_part * jax.nn.sigmoid(1.702 * gate_part)).astype(jnp.bfloat16)
    projected = jnp.dot(activated, second_weight, preferred_element_type=jnp.float32) + second_bias.astype(jnp.float32)
    return projected.astype(jnp.bfloat16)

def rotary_heads(projected, token_positions):
    half_dim = projected.shape[-1] // 2
    frequency = jnp.power(jnp.float32(150000.0), -2.0 * jnp.arange(half_dim, dtype=jnp.float32) / (2 * half_dim))
    angles = token_positions.astype(jnp.float32)[:, None] * frequency[None, :]
    cosine = jnp.cos(angles)[:, None, :]
    sine_part = jnp.sin(angles)[:, None, :]
    first_half = projected[..., :half_dim]
    second_half = projected[..., half_dim:]
    return jnp.concatenate([first_half * cosine - second_half * sine_part, second_half * cosine + first_half * sine_part], axis=-1)

def band_block(query_block, key_block, value_block, query_pos, key_pos, sink_scores):
    scale = 1.0 / math.sqrt(query_block.shape[-1])
    scores = jnp.einsum('qhgd,khd->hgqk', query_block.astype(jnp.float32), key_block.astype(jnp.float32)) * scale
    distance = query_pos[:, None] - key_pos[None, :]
    allowed = (distance >= 0) & (distance < WINDOW_LENGTH) & (key_pos[None, :] >= 0)
    masked = jnp.where(allowed, scores, -jnp.inf)
    top_score = jnp.maximum(lax.optimization_barrier(jnp.max(masked, axis=-1)), sink_scores[:, :, None])
    weights = jnp.where(allowed, jnp.exp(scores - top_score[..., None]), 0.0)
    total = jnp.exp(sink_scores[:, :, None] - top_score) + lax.optimization_barrier(jnp.sum(weights, axis=-1))
    probs = (weights / total[..., None]).astype(jnp.bfloat16)
    mixed = jnp.einsum('hgqk,khd->qhgd', probs.astype(jnp.float32), value_block.astype(jnp.float32))
    return mixed.astype(jnp.bfloat16)

def reference(tokens, route_ids, route_level, gate_up_codes, gate_up_scale, gate_up_bias, down_codes, down_scale, down_bias, attn_gain, query_weight, key_matrix, value_matrix, sinks):
    flat_ids = route_ids.reshape(-1).astype(jnp.int32)
    one_hot = (flat_ids[:, None] == jnp.arange(EXPERTS, dtype=jnp.int32)[None, :]).astype(jnp.int32)
    ranks = lax.optimization_barrier(jnp.sum((jnp.cumsum(one_hot, axis=0) - 1) * one_hot, axis=1)).astype(jnp.int32)
    owners = (jnp.arange(TOKEN_COUNT * TOPK, dtype=jnp.int32) // TOPK).astype(jnp.int32)
    capacity = TOKEN_COUNT // TOK_DEV * MOST
    slot_token = jnp.zeros((EXPERTS, capacity), jnp.int32).at[flat_ids, ranks].set(owners)

    def one_expert(packed):
        up_words, up_exponents, up_bias, low_words, low_exponents, low_bias, chosen = packed
        first_weight = decode_weights(up_words, up_exponents)
        second_weight = decode_weights(low_words, low_exponents)
        return expert_rows(tokens[chosen], first_weight, second_weight, up_bias, low_bias)
    served = lax.map(one_expert, (gate_up_codes, gate_up_scale, gate_up_bias, down_codes, down_scale, down_bias, slot_token))
    gathered = served[flat_ids, ranks].reshape(TOKEN_COUNT, TOPK, MODEL_FEATURES).astype(jnp.float32)
    raised = jnp.exp(route_level.astype(jnp.float32) / 4.0)
    route_prob = raised / lax.optimization_barrier(jnp.sum(raised, axis=-1, keepdims=True))
    mixture = lax.optimization_barrier(jnp.sum(route_prob[..., None] * gathered, axis=1))
    block_out = (tokens.astype(jnp.float32) + mixture).astype(jnp.bfloat16)
    widened = block_out.astype(jnp.float32)
    squares = lax.optimization_barrier(jnp.mean(widened * widened, axis=-1, keepdims=True))
    normalized_input = (widened * lax.rsqrt(squares + 1e-05) * attn_gain.astype(jnp.float32)).astype(jnp.bfloat16)
    token_positions = jnp.arange(TOKEN_COUNT, dtype=jnp.int32)
    query_rows = rotary_heads(jnp.dot(normalized_input, query_weight, preferred_element_type=jnp.float32).reshape(TOKEN_COUNT, QUERY_HEAD_COUNT, HEAD_SIZE), token_positions).astype(jnp.bfloat16)
    every_key_row = rotary_heads(jnp.dot(normalized_input, key_matrix, preferred_element_type=jnp.float32).reshape(TOKEN_COUNT, KEY_VALUE_HEADS, HEAD_SIZE), token_positions).astype(jnp.bfloat16)
    every_value_row = jnp.dot(normalized_input, value_matrix, preferred_element_type=jnp.float32).astype(jnp.bfloat16).reshape(TOKEN_COUNT, KEY_VALUE_HEADS, HEAD_SIZE)
    key_rows_padded = jnp.concatenate([jnp.zeros((WINDOW_LENGTH, KEY_VALUE_HEADS, HEAD_SIZE), jnp.bfloat16), every_key_row], axis=0)
    value_rows_padded = jnp.concatenate([jnp.zeros((WINDOW_LENGTH, KEY_VALUE_HEADS, HEAD_SIZE), jnp.bfloat16), every_value_row], axis=0)
    grouped_queries = query_rows.reshape(TOKEN_COUNT // WINDOW_LENGTH, WINDOW_LENGTH, KEY_VALUE_HEADS, QUERY_HEAD_COUNT // KEY_VALUE_HEADS, HEAD_SIZE)
    sink_scores = sinks.astype(jnp.float32).reshape(KEY_VALUE_HEADS, QUERY_HEAD_COUNT // KEY_VALUE_HEADS)

    def one_block(block_index):
        start = (block_index * WINDOW_LENGTH).astype(jnp.int32)
        key_block = lax.dynamic_slice_in_dim(key_rows_padded, start, 2 * WINDOW_LENGTH, 0)
        value_block = lax.dynamic_slice_in_dim(value_rows_padded, start, 2 * WINDOW_LENGTH, 0)
        query_pos = start + jnp.arange(WINDOW_LENGTH, dtype=jnp.int32)
        key_pos = start - WINDOW_LENGTH + jnp.arange(2 * WINDOW_LENGTH, dtype=jnp.int32)
        return band_block(grouped_queries[block_index], key_block, value_block, query_pos, key_pos, sink_scores)
    attended = lax.map(one_block, jnp.arange(TOKEN_COUNT // WINDOW_LENGTH, dtype=jnp.int32)).reshape(TOKEN_COUNT, QUERY_HEAD_COUNT * HEAD_SIZE)
    return (block_out, attended)
```

```python
import functools

import jax
import jax.numpy as jnp
from jax import lax
from jax.experimental import pallas as pl
from jax.experimental.pallas import tpu as pltpu
from jax.sharding import PartitionSpec as P

HEAD_SIZE = 64
WINDOW_LENGTH = 128
MOST = 64
WIDE = 1536
CHUNKS = 3
RETURN_SCALE = 8.0
VMEM_LIMIT = 56 * 1024 * 1024
F32 = jnp.float32
BF16 = jnp.bfloat16


def twice_fp4(words, field_index):
    low = jnp.bitwise_and(jnp.right_shift(words, 4 * field_index), 7).astype(F32)
    return jnp.maximum(jnp.maximum(low, 2.0 * low - 4.0), 4.0 * low - 16.0)


def signed_scale(words, field_index, scale):
    return jnp.where(jnp.bitwise_and(words, 8 << (4 * field_index)) != 0, -scale, scale)


def decode_up_kernel(codes_ref, scale_ref, out_ref):
    for block in range(9):
        words = codes_ref[32 * block : 32 * block + 32, :]
        for place, field_index in enumerate((0, 2, 1, 3)):
            scale = scale_ref[0, 0, 4 * block + place : 4 * block + place + 1, :]
            value = twice_fp4(words, field_index) * signed_scale(words, field_index, scale)
            out_ref[0, 32 * block : 32 * block + 32, 256 * place : 256 * place + 256] = (
                value.astype(BF16)
            )


def decode_up(codes, scale):
    rows, words = codes.shape
    return pl.pallas_call(
        decode_up_kernel,
        grid=(CHUNKS, 5),
        in_specs=[
            pl.BlockSpec((288, 256), lambda b, r: (r, b)),
            pl.BlockSpec((1, 1, 36, 256), lambda b, r: (r, b, 0, 0)),
        ],
        out_specs=pl.BlockSpec((1, 288, 1024), lambda b, r: (b, r, 0)),
        out_shape=jax.ShapeDtypeStruct((CHUNKS, rows, 1024), BF16),
        compiler_params=pltpu.CompilerParams(vmem_limit_bytes=VMEM_LIMIT),
        cost_estimate=pl.CostEstimate(flops=60_000_000, bytes_accessed=14_000_000, transcendentals=0),
        name="decode_up",
    )(codes, scale)


def decode_down_kernel(left_ref, middle_ref, right_ref, scale_ref, out_ref):
    source = lax.broadcasted_iota(jnp.int32, (512, 512), 0)
    target = lax.broadcasted_iota(jnp.int32, (512, 512), 1)
    wanted = 4 * jnp.bitwise_and(source, 127) + jnp.right_shift(source, 7)
    spread = jnp.where(target == wanted, 1.0, 0.0).astype(BF16)
    for parity in range(2):
        for part, codes_ref in enumerate((left_ref, middle_ref, right_ref)):
            piece = codes_ref[pl.ds(parity, 256, 2), :]
            fields = []
            for field_index in range(4):
                size = twice_fp4(piece, field_index)
                value = jnp.where(
                    jnp.bitwise_and(piece, 8 << (4 * field_index)) != 0, -size, size
                )
                fields.append(value.astype(BF16))
            natural = jnp.dot(
                jnp.concatenate(fields, axis=1), spread, preferred_element_type=F32
            )
            for block in range(16):
                scale = scale_ref[block : block + 1, 512 * part : 512 * part + 512]
                row = 256 * parity + 16 * block
                out_ref[0, row : row + 16, 512 * part : 512 * part + 512] = (
                    natural[16 * block : 16 * block + 16] * scale
                ).astype(BF16)


def decode_down(codes, scale):
    return pl.pallas_call(
        decode_down_kernel,
        grid=(CHUNKS,),
        in_specs=[
            pl.BlockSpec((512, 128), lambda b: (b, 0)),
            pl.BlockSpec((512, 128), lambda b: (b, 1)),
            pl.BlockSpec((512, 128), lambda b: (b, 2)),
            pl.BlockSpec((16, WIDE), lambda b: (b, 0)),
        ],
        out_specs=pl.BlockSpec((1, 512, WIDE), lambda b: (b, 0, 0)),
        out_shape=jax.ShapeDtypeStruct((CHUNKS, 512, WIDE), BF16),
        compiler_params=pltpu.CompilerParams(vmem_limit_bytes=VMEM_LIMIT),
        cost_estimate=pl.CostEstimate(flops=60_000_000, bytes_accessed=7_000_000, transcendentals=0),
        name="decode_down",
    )(codes, codes, codes, scale)


def pack_kernel(tokens_ref, ids_ref, level_ref, out_ref):
    out_ref[:, :1440] = tokens_ref[...]
    out_ref[:, 1440:1444] = ids_ref[...].astype(F32).astype(BF16)
    out_ref[:, 1444:1448] = level_ref[...].astype(F32).astype(BF16)
    out_ref[:, 1448:] = jnp.zeros((128, WIDE - 1448), BF16)


def pack(tokens, route_ids, route_level):
    return pl.pallas_call(
        pack_kernel,
        out_shape=jax.ShapeDtypeStruct((128, WIDE), BF16),
        compiler_params=pltpu.CompilerParams(vmem_limit_bytes=VMEM_LIMIT),
        name="pack",
    )(tokens, route_ids, route_level)


def earlier_rows():
    row = lax.broadcasted_iota(jnp.int32, (128, 128), 0)
    column = lax.broadcasted_iota(jnp.int32, (128, 128), 1)
    return jnp.where(column < row, 1.0, 0.0).astype(BF16)


def expert_kernel(shard_count, place_ref, *refs):
    shards = refs[:shard_count]
    (
        first_ref,
        second_ref,
        first_bias_ref,
        second_bias_ref,
        near_ref,
        other_ref,
        rows_ref,
        total_ref,
    ) = refs[shard_count:]
    chunk = pl.program_id(0)
    half = shard_count // 2 * MOST

    @pl.when(chunk == 0)
    def _():
        before = earlier_rows()
        lane = lax.broadcasted_iota(jnp.int32, (128, 128), 1)
        slot = jnp.bitwise_and(lane, MOST - 1).astype(F32)
        lower = lane < MOST
        expert = place_ref[shard_count].astype(F32)
        for j in range(0, shard_count, 2):
            picks = []
            for i in range(2):
                meta = shards[j + i][:, 1408:1536].astype(F32)
                named = jnp.zeros((128, 1), F32)
                for choice in range(4):
                    named = named + jnp.where(
                        meta[:, 32 + choice : 33 + choice] == expert, 1.0, 0.0
                    )
                spread = jnp.broadcast_to(named, (128, 128))
                rank = jnp.dot(before, spread.astype(BF16), preferred_element_type=F32)
                pick = jnp.where((rank == slot) & (spread > 0.0), 1.0, 0.0)
                pick = jnp.where(lower if i == 0 else jnp.logical_not(lower), pick, 0.0)
                picks.append(pick.astype(BF16))
            rows = lax.dot_general(
                jnp.concatenate(picks, axis=0),
                jnp.concatenate([shards[j][...], shards[j + 1][...]], axis=0),
                (((0,), (0,)), ((), ())),
                preferred_element_type=F32,
            )
            rows_ref[MOST * j : MOST * j + 2 * MOST, :] = rows.astype(BF16)

    pre = jnp.dot(rows_ref[:, :1440], first_ref[0], preferred_element_type=F32)
    pre = pre + first_bias_ref[chunk]
    gate = jnp.minimum(pre[:, :512], 7.0)
    up = jnp.clip(pre[:, 512:], -7.0, 7.0)
    activated = ((up + 1.0) * gate * (0.5 + 0.5 * jnp.tanh(0.851 * gate))).astype(BF16)
    product = jnp.dot(activated, second_ref[0], preferred_element_type=F32)

    @pl.when(chunk == 0)
    def _():
        total_ref[...] = product + second_bias_ref[...]

    @pl.when(chunk == 1)
    def _():
        total_ref[...] += product

    @pl.when(chunk == CHUNKS - 1)
    def _():
        done = (total_ref[...] + product).astype(BF16)
        near_ref[...] = done[:half]
        other_ref[...] = done[half:]


def run_experts(shards, expert, gathered, first, second, first_bias, second_bias):
    count = len(shards)
    rows = count * MOST
    place = jnp.stack(shards + [expert]).astype(jnp.int32)

    def shard_spec(j):
        return pl.BlockSpec((128, WIDE), lambda b, place: (place[j], 0))

    half = jax.ShapeDtypeStruct((rows // 2, WIDE), BF16)
    half_spec = pl.BlockSpec((rows // 2, WIDE), lambda b, place: (0, 0))
    return pl.pallas_call(
        functools.partial(expert_kernel, count),
        grid_spec=pltpu.PrefetchScalarGridSpec(
            num_scalar_prefetch=1,
            grid=(CHUNKS,),
            in_specs=[shard_spec(j) for j in range(count)]
            + [
                pl.BlockSpec((1, 1440, 1024), lambda b, place: (b, 0, 0)),
                pl.BlockSpec((1, 512, WIDE), lambda b, place: (b, 0, 0)),
                pl.BlockSpec((CHUNKS, 1, 1024), lambda b, place: (0, 0, 0)),
                pl.BlockSpec((1, WIDE), lambda b, place: (0, 0)),
            ],
            out_specs=[half_spec, half_spec],
            scratch_shapes=[pltpu.VMEM((rows, WIDE), BF16), pltpu.VMEM((rows, WIDE), F32)],
        ),
        out_shape=[half, half],
        compiler_params=pltpu.CompilerParams(vmem_limit_bytes=VMEM_LIMIT),
        cost_estimate=pl.CostEstimate(
            flops=2 * rows * 1440 * 4320, bytes_accessed=15_000_000, transcendentals=0
        ),
        name="experts",
    )(place, *([gathered] * count), first, second, first_bias, second_bias)


def combine_kernel(shard_count, place_ref, *refs):
    metas = refs[:shard_count]
    near_ref, other_ref, out_ref = refs[shard_count:]
    before = earlier_rows()
    lane = lax.broadcasted_iota(jnp.int32, (128, 128), 1)
    slot = jnp.bitwise_and(lane, MOST - 1).astype(F32)
    expert = jnp.where(lane < MOST, place_ref[shard_count], place_ref[shard_count + 1]).astype(F32)
    for j in range(shard_count):
        meta = metas[j][...].astype(F32)
        raised = jnp.exp(meta / 4.0)
        named = jnp.zeros((128, 128), F32)
        chosen = jnp.zeros((128, 128), F32)
        whole = jnp.zeros((128, 1), F32)
        for choice in range(4):
            same = meta[:, 32 + choice : 33 + choice] == expert
            level = raised[:, 36 + choice : 37 + choice]
            named = jnp.where(same, 1.0, named)
            chosen = jnp.where(same, level, chosen)
            whole = whole + level
        rank = jnp.dot(before, named.astype(BF16), preferred_element_type=F32)
        weight = jnp.where((rank == slot) & (named > 0.0), chosen / whole * RETURN_SCALE, 0.0)
        high = weight.astype(BF16)
        low = (weight - high.astype(F32)).astype(BF16)
        near = near_ref[MOST * j : MOST * j + MOST, :]
        other = other_ref[MOST * j : MOST * j + MOST, :]
        out_ref[j] = jnp.dot(
            jnp.concatenate([high, low], axis=1),
            jnp.concatenate([near, other, near, other], axis=0),
            preferred_element_type=F32,
        )


def combine(shards, experts, gathered, near, other):
    count = len(shards)
    place = jnp.stack(shards + experts).astype(jnp.int32)

    def meta_spec(j):
        return pl.BlockSpec((128, 128), lambda i, place: (place[j], 11))

    rows_spec = pl.BlockSpec((count * MOST, WIDE), lambda i, place: (0, 0))
    return pl.pallas_call(
        functools.partial(combine_kernel, count),
        grid_spec=pltpu.PrefetchScalarGridSpec(
            num_scalar_prefetch=1,
            grid=(1,),
            in_specs=[meta_spec(j) for j in range(count)] + [rows_spec, rows_spec],
            out_specs=pl.BlockSpec((count, 128, WIDE), lambda i, place: (0, 0, 0)),
        ),
        out_shape=jax.ShapeDtypeStruct((count, 128, WIDE), F32),
        compiler_params=pltpu.CompilerParams(vmem_limit_bytes=VMEM_LIMIT),
        cost_estimate=pl.CostEstimate(
            flops=2 * count * 128 * 256 * WIDE, bytes_accessed=1_500_000 * count, transcendentals=0
        ),
        name="combine",
    )(place, *([gathered] * count), near, other)


def turned(block, cosine, sine_part):
    width = block.shape[1]
    lane = lax.broadcasted_iota(jnp.int32, block.shape, 1)
    first = jnp.bitwise_and(lane, 63) < 32
    swapped = jnp.where(first, pltpu.roll(block, width - 32, 1), pltpu.roll(block, 32, 1))
    copies = width // 128
    cosine = jnp.concatenate([cosine] * copies, axis=1)
    sine_part = jnp.concatenate([sine_part] * copies, axis=1)
    return block * cosine + swapped * sine_part


def mix_kernel(
    tokens_ref, mixture_ref, gain_ref, key_ref, value_ref, cos_ref, sin_ref, out_ref, normed_ref, kv_ref
):
    block_out = (tokens_ref[...].astype(F32) + mixture_ref[...]).astype(BF16)
    out_ref[...] = block_out
    widened = block_out.astype(F32)
    squares = jnp.sum(widened * widened, axis=1, keepdims=True) / 1440.0
    normed = (widened * lax.rsqrt(squares + 1e-05) * gain_ref[...].astype(F32)).astype(BF16)
    normed_ref[...] = normed
    keys = jnp.dot(normed, key_ref[...], preferred_element_type=F32)
    kv_ref[:, :256] = turned(keys, cos_ref[...], sin_ref[...]).astype(BF16)
    kv_ref[:, 256:] = jnp.dot(normed, value_ref[...], preferred_element_type=F32).astype(BF16)


def mix(tokens, mixture, gain, key_matrix, value_matrix, cosine, sine_part):
    return pl.pallas_call(
        mix_kernel,
        out_shape=[
            jax.ShapeDtypeStruct((128, 1440), BF16),
            jax.ShapeDtypeStruct((128, 1440), BF16),
            jax.ShapeDtypeStruct((128, 512), BF16),
        ],
        compiler_params=pltpu.CompilerParams(vmem_limit_bytes=VMEM_LIMIT),
        cost_estimate=pl.CostEstimate(
            flops=2 * 128 * 1440 * 512, bytes_accessed=3_000_000, transcendentals=0
        ),
        name="mix",
    )(tokens, mixture, gain, key_matrix, value_matrix, cosine, sine_part)


def queries_kernel(normed_ref, weight_ref, cos_ref, sin_ref, out_ref):
    projected = jnp.dot(normed_ref[...], weight_ref[...], preferred_element_type=F32)
    rotated = turned(projected, cos_ref[...], sin_ref[...])
    scaled = (rotated.astype(BF16).astype(F32) * 0.125).astype(BF16)
    for pair in range(4):
        out_ref[0, 128 * pair : 128 * pair + 128, :] = scaled[:, 128 * pair : 128 * pair + 128]


def queries(normed, weight, cosine, sine_part):
    return pl.pallas_call(
        queries_kernel,
        grid=(4,),
        in_specs=[
            pl.BlockSpec((128, 1440), lambda g: (0, 0)),
            pl.BlockSpec((1440, 512), lambda g: (0, g)),
            pl.BlockSpec((128, 128), lambda g: (0, 0)),
            pl.BlockSpec((128, 128), lambda g: (0, 0)),
        ],
        out_specs=pl.BlockSpec((1, 512, 128), lambda g: (g, 0, 0)),
        out_shape=jax.ShapeDtypeStruct((4, 512, 128), BF16),
        compiler_params=pltpu.CompilerParams(vmem_limit_bytes=VMEM_LIMIT),
        cost_estimate=pl.CostEstimate(
            flops=2 * 128 * 1440 * 2048, bytes_accessed=7_000_000, transcendentals=0
        ),
        name="queries",
    )(normed, weight, cosine, sine_part)


def attend_kernel(index_ref, sinks_ref, queries_ref, own_ref, halo_ref, out_ref):
    lane = lax.broadcasted_iota(jnp.int32, (128, 128), 1)
    lower = lane < 64

    def doubled(block, odd):
        block = block.astype(F32)
        if odd:
            high = jnp.where(lower, 0.0, block)
            low = pltpu.roll(high, 64, 1)
        else:
            low = jnp.where(lower, block, 0.0)
            high = pltpu.roll(low, 64, 1)
        return jnp.concatenate([low, high], axis=0).astype(BF16)

    row = lax.broadcasted_iota(jnp.int32, (128, 256), 0)
    column = jnp.bitwise_and(lax.broadcasted_iota(jnp.int32, (128, 256), 1), 127)
    mine = column <= row
    allowed = mine | jnp.broadcast_to(index_ref[0] > 0, mine.shape)
    for group in range(4):
        start = 128 * (group // 2)
        odd = group % 2 == 1
        query = queries_ref[group]
        across = (((1,), (1,)), ((), ()))
        here = lax.dot_general(
            query, doubled(own_ref[:, start : start + 128], odd), across, preferred_element_type=F32
        )
        there = lax.dot_general(
            query, doubled(halo_ref[:, start : start + 128], odd), across, preferred_element_type=F32
        )
        here_probs = []
        there_probs = []
        for pair in range(4):
            rows = slice(128 * pair, 128 * pair + 128)
            scores = jnp.where(mine, here[rows], there[rows])
            scores = jnp.where(allowed, scores, -1e30)
            halves = []
            for side in range(2):
                part = scores[:, 128 * side : 128 * side + 128]
                sink = sinks_ref[8 * group + 2 * pair + side]
                top = jnp.maximum(jnp.max(part, axis=1, keepdims=True), sink)
                weights = jnp.exp(part - top)
                whole = jnp.exp(sink - top) + jnp.sum(weights, axis=1, keepdims=True)
                halves.append(weights * (1.0 / whole))
            probs = jnp.where(allowed, jnp.concatenate(halves, axis=1), 0.0)
            here_probs.append(jnp.where(mine, probs, 0.0).astype(BF16))
            there_probs.append(jnp.where(mine, 0.0, probs).astype(BF16))
        mixed = jnp.dot(
            jnp.concatenate(here_probs, axis=0),
            doubled(own_ref[:, 256 + start : 384 + start], odd),
            preferred_element_type=F32,
        ) + jnp.dot(
            jnp.concatenate(there_probs, axis=0),
            doubled(halo_ref[:, 256 + start : 384 + start], odd),
            preferred_element_type=F32,
        )
        for pair in range(4):
            place = 512 * group + 128 * pair
            out_ref[:, place : place + 128] = mixed[128 * pair : 128 * pair + 128].astype(BF16)


def attend(index, sinks, query, own, halo):
    return pl.pallas_call(
        attend_kernel,
        in_specs=[
            pl.BlockSpec(memory_space=pltpu.SMEM),
            pl.BlockSpec(memory_space=pltpu.SMEM),
            pl.BlockSpec(memory_space=pltpu.VMEM),
            pl.BlockSpec(memory_space=pltpu.VMEM),
            pl.BlockSpec(memory_space=pltpu.VMEM),
        ],
        out_specs=pl.BlockSpec(memory_space=pltpu.VMEM),
        out_shape=jax.ShapeDtypeStruct((128, 2048), BF16),
        compiler_params=pltpu.CompilerParams(vmem_limit_bytes=VMEM_LIMIT),
        cost_estimate=pl.CostEstimate(
            flops=2 * 32 * 128 * 256 * 128, bytes_accessed=1_500_000, transcendentals=1_000_000
        ),
        name="attend",
    )(index, sinks, query, own, halo)


def by_field(rows):
    count = rows.shape[0]
    padded = jnp.pad(rows, ((0, 0), (0, 3072 - rows.shape[1]))).reshape(count, 6, 512)
    source = lax.broadcasted_iota(jnp.int32, (512, 512), 0)
    target = lax.broadcasted_iota(jnp.int32, (512, 512), 1)
    wanted = 128 * (source % 4) + source // 4
    spread = jnp.where(target == wanted, 1.0, 0.0).astype(BF16)
    sorted_rows = jnp.einsum("rbs,st->rbt", padded, spread, preferred_element_type=F32)
    sorted_rows = sorted_rows.reshape(count, CHUNKS, 2, 4, 128)
    places = [sorted_rows[:, :, :, field] for field in (0, 2, 1, 3)]
    return jnp.stack(places, axis=2).reshape(count, CHUNKS, 4, 256)


def body(
    tokens,
    route_ids,
    route_level,
    gate_up_codes,
    gate_up_scale,
    gate_up_bias,
    down_codes,
    down_scale,
    down_bias,
    attn_gain,
    query_weight,
    key_matrix,
    value_matrix,
    sinks,
):
    own_tokens, width = tokens.shape
    group_size = lax.axis_size("expert")
    chips = group_size // 2
    device_index = lax.axis_index("expert")
    chip = device_index // 2
    core = device_index % 2
    side = 2 * core - 1

    packed = pack(tokens, route_ids, route_level)
    gathered = lax.all_gather(packed, "expert", axis=0, tiled=True)

    up_scale = jnp.exp2((gate_up_scale[0] - 128).astype(F32)).astype(BF16)
    by_place = by_field(jnp.concatenate([up_scale, gate_up_bias], axis=0))
    up_scales = (
        by_place[:45].reshape(5, 9, CHUNKS, 4, 256).transpose(0, 2, 1, 3, 4)
    ).reshape(5, CHUNKS, 36, 256)
    first_bias = by_place[45].reshape(CHUNKS, 1, 1024)
    down_scales = jnp.pad(
        jnp.exp2((down_scale[0] - 128).astype(F32)), ((0, 3), (0, WIDE - width))
    )
    second_bias = jnp.pad(down_bias.astype(F32), ((0, 0), (0, WIDE - width)))
    second = decode_down(down_codes[0], down_scales)
    first = decode_up(gate_up_codes[0], up_scales)

    half_dim = HEAD_SIZE // 2
    frequency = jnp.power(
        jnp.float32(150000.0), -2.0 * jnp.arange(half_dim, dtype=F32) / (2 * half_dim)
    )
    token_positions = device_index * own_tokens + jnp.arange(own_tokens, dtype=jnp.int32)
    angles = token_positions.astype(F32)[:, None] * frequency[None, :]
    cosine = jnp.tile(jnp.cos(angles), (1, 4))
    sine_part = jnp.sin(angles)
    sine_part = jnp.concatenate([-sine_part, sine_part, -sine_part, sine_part], axis=1)

    def shard(toward, distance, column):
        return ((chip + toward * distance) % chips) * 2 + column

    far = chips // 2

    def order(toward, column, distances):
        chosen = []
        for distance in distances:
            chosen.append(shard(toward, distance, column))
            if 0 < distance < far:
                chosen.append(shard(toward, distance, 1 - column))
        return chosen

    partner = [(i, i ^ 1) for i in range(group_size)]
    experts = [device_index, device_index + 1 - 2 * core]

    def serve(distances):
        mine = order(side, core, distances)
        others = order(-side, 1 - core, distances)
        near, other = run_experts(
            mine + others, device_index, gathered, first, second, first_bias, second_bias
        )
        return combine(mine, experts, gathered, near, lax.ppermute(other, "expert", partner))

    early = serve([far, far - 1])
    late = serve(list(range(far - 2, -1, -1)))

    def onward(block, across):
        route = []
        for i in range(group_size):
            step = 2 if i % 2 else -2
            goal = (i + step) % group_size
            route.append((i, goal ^ 1 if across else goal))
        return lax.ppermute(block.astype(jnp.float16), "expert", route).astype(F32)

    moving = onward(early[0], False)
    moving = jnp.concatenate([early[1] + moving, early[2]], axis=0)
    for distance in range(far - 2, 0, -1):
        here = 2 * (far - 2 - distance)
        moving = onward(moving, False)
        moving = late[here : here + 2].reshape(2 * own_tokens, WIDE) + moving
    from_one = onward(moving[:own_tokens], False)
    from_other = onward(moving[own_tokens:], True)
    mixture = (late[2 * (far - 2)] + from_one + from_other)[:, :width] * (1.0 / RETURN_SCALE)

    block_out, normed, own_kv = mix(
        tokens, mixture, attn_gain[None], key_matrix, value_matrix, cosine, sine_part
    )
    ahead = [(i, i + 1) for i in range(group_size - 1)]
    halo_kv = lax.ppermute(own_kv, "expert", ahead)
    query = queries(normed, query_weight, cosine, sine_part)
    attended = attend(device_index.reshape(1), sinks, query, own_kv, halo_kv)
    return (block_out, attended)


def solution(mesh):
    in_specs = (
        P(("dp", "expert"), None),
        P(("dp", "expert"), None),
        P(("dp", "expert"), None),
        P("expert", None, None),
        P("expert", None, None),
        P("expert", None),
        P("expert", None, None),
        P("expert", None, None),
        P("expert", None),
        P(),
        P(),
        P(),
        P(),
        P(),
    )
    out_specs = (P(("dp", "expert"), None), P(("dp", "expert"), None))
    return jax.shard_map(body, mesh=mesh, in_specs=in_specs, out_specs=out_specs, check_vma=False)
```

```python
import functools

import jax
import jax.numpy as jnp
from jax import lax
from jax.experimental import pallas as pl
from jax.experimental.pallas import tpu as pltpu
from jax.sharding import PartitionSpec as P

HEAD_SIZE = 64
WINDOW_LENGTH = 128
MOST = 64
WIDE = 1536
CHUNKS = 3
RETURN_SCALE = 8.0
LARGE_LIMIT = 56 * 1024 * 1024
VMEM_LIMIT = 40 * 1024 * 1024
SMALL_LIMIT = 24 * 1024 * 1024
F32 = jnp.float32
BF16 = jnp.bfloat16


def twice_fp4(words, field_index):
    field = jnp.bitwise_and(jnp.right_shift(words, 4 * field_index), 15).astype(F32).astype(BF16)
    negative = field >= 8
    low = jnp.where(negative, field - 8, field)
    return negative, jnp.maximum(jnp.maximum(low, 2 * low - 4), 4 * low - 16)


def power_of_two(exponents, least, valid):
    step = exponents - least
    scale = jnp.where(step == 0, 1.0, jnp.where(step == 1, 2.0, jnp.where(step == 2, 4.0, 8.0)))
    return jnp.where(valid, scale * 2.0 ** (least - 128), 0.0)


def decode_up_kernel(codes_ref, exponent_ref, bias_ref, out_ref, bias_out_ref, scale_ref):
    source = lax.broadcasted_iota(jnp.int32, (512, 512), 0)
    target = lax.broadcasted_iota(jnp.int32, (512, 512), 1)
    wanted = 128 * jnp.bitwise_and(source, 3) + jnp.right_shift(source, 2)
    spread = jnp.where(target == wanted, 1.0, 0.0).astype(BF16)
    for half in range(2):
        lanes = slice(512 * half, 512 * half + 512)
        left = 2880 - 1024 * pl.program_id(0) - 512 * half
        column = lax.broadcasted_iota(jnp.int32, (45, 512), 1)
        scale = power_of_two(exponent_ref[:, lanes], 119, column < left)
        scale = jnp.dot(scale.astype(BF16), spread, preferred_element_type=F32)
        bias = jnp.where(column[:1] < left, bias_ref[:, lanes].astype(F32), 0.0)
        bias = jnp.broadcast_to(bias, (16, 512)).astype(BF16)
        bias = jnp.dot(bias, spread, preferred_element_type=F32)
        for place, field_index in enumerate((0, 2, 1, 3)):
            taken = slice(128 * field_index, 128 * field_index + 128)
            given = slice(256 * place + 128 * half, 256 * place + 128 * half + 128)
            scale_ref[:45, given] = scale[:, taken]
            bias_out_ref[0, :, given] = bias[:1, taken]
    for block in range(45):
        words = codes_ref[32 * block : 32 * block + 32, :]
        for place, field_index in enumerate((0, 2, 1, 3)):
            lanes = slice(256 * place, 256 * place + 256)
            scale = scale_ref[block : block + 1, lanes]
            negative, size = twice_fp4(words, field_index)
            scale = jnp.broadcast_to(scale.astype(BF16), size.shape)
            out_ref[0, 32 * block : 32 * block + 32, lanes] = size * jnp.where(
                negative, -scale, scale
            )


def decode_up(codes, exponents, bias):
    rows = codes.shape[0]
    return pl.pallas_call(
        decode_up_kernel,
        grid=(CHUNKS,),
        in_specs=[
            pl.BlockSpec((1440, 256), lambda b: (0, b)),
            pl.BlockSpec((45, 1024), lambda b: (0, b)),
            pl.BlockSpec((1, 1024), lambda b: (0, b)),
        ],
        out_specs=[
            pl.BlockSpec((1, 1440, 1024), lambda b: (b, 0, 0)),
            pl.BlockSpec((1, 1, 1024), lambda b: (b, 0, 0)),
        ],
        out_shape=[
            jax.ShapeDtypeStruct((CHUNKS, rows, 1024), BF16),
            jax.ShapeDtypeStruct((CHUNKS, 1, 1024), F32),
        ],
        scratch_shapes=[pltpu.VMEM((48, 1024), F32)],
        compiler_params=pltpu.CompilerParams(vmem_limit_bytes=LARGE_LIMIT),
        cost_estimate=pl.CostEstimate(flops=60_000_000, bytes_accessed=30_000_000, transcendentals=0),
        name="decode_up",
    )(codes, exponents, bias)


def decode_down_kernel(
    left_ref, middle_ref, right_ref, left_exp_ref, middle_exp_ref, right_exp_ref, out_ref
):
    row = lax.broadcasted_iota(jnp.int32, (16, 512), 0) + 16 * pl.program_id(0)
    column = lax.broadcasted_iota(jnp.int32, (16, 512), 1)
    scales = [
        power_of_two(exponent_ref[...], 117, (row < 45) & (column < 1440 - 512 * part))
        for part, exponent_ref in enumerate((left_exp_ref, middle_exp_ref, right_exp_ref))
    ]
    source = lax.broadcasted_iota(jnp.int32, (512, 512), 0)
    target = lax.broadcasted_iota(jnp.int32, (512, 512), 1)
    wanted = 4 * jnp.bitwise_and(source, 127) + jnp.right_shift(source, 7)
    spread = jnp.where(target == wanted, 1.0, 0.0).astype(BF16)
    for parity in range(2):
        for part, codes_ref in enumerate((left_ref, middle_ref, right_ref)):
            piece = codes_ref[pl.ds(parity, 256, 2), :]
            fields = []
            for field_index in range(4):
                negative, size = twice_fp4(piece, field_index)
                fields.append(jnp.where(negative, -size, size))
            natural = jnp.dot(
                jnp.concatenate(fields, axis=1), spread, preferred_element_type=F32
            )
            for block in range(16):
                scale = scales[part][block : block + 1, :]
                row = 256 * parity + 16 * block
                out_ref[0, row : row + 16, 512 * part : 512 * part + 512] = (
                    natural[16 * block : 16 * block + 16] * scale
                ).astype(BF16)


def decode_down(codes, exponents):
    return pl.pallas_call(
        decode_down_kernel,
        grid=(CHUNKS,),
        in_specs=[
            pl.BlockSpec((512, 128), lambda b: (b, 0)),
            pl.BlockSpec((512, 128), lambda b: (b, 1)),
            pl.BlockSpec((512, 128), lambda b: (b, 2)),
            pl.BlockSpec((16, 512), lambda b: (b, 0)),
            pl.BlockSpec((16, 512), lambda b: (b, 1)),
            pl.BlockSpec((16, 512), lambda b: (b, 2)),
        ],
        out_specs=pl.BlockSpec((1, 512, WIDE), lambda b: (b, 0, 0)),
        out_shape=jax.ShapeDtypeStruct((CHUNKS, 512, WIDE), BF16),
        compiler_params=pltpu.CompilerParams(vmem_limit_bytes=VMEM_LIMIT),
        cost_estimate=pl.CostEstimate(flops=60_000_000, bytes_accessed=20_000_000, transcendentals=0),
        name="decode_down",
    )(codes, codes, codes, exponents, exponents, exponents)


def pack_kernel(tokens_ref, ids_ref, level_ref, out_ref):
    for place in range(11):
        block = tokens_ref[128 * place : 128 * place + 128, :].astype(F32)
        out_ref[:, 128 * place : 128 * place + 128] = block.T.astype(BF16)
    expert = lax.broadcasted_iota(jnp.int32, (16, 128), 0)
    named = jnp.zeros((16, 128), F32)
    chosen = jnp.zeros((16, 128), F32)
    whole = jnp.zeros((1, 128), F32)
    for choice in range(4):
        raised = jnp.exp(level_ref[choice : choice + 1, :].astype(F32) / 4.0)
        same = ids_ref[choice : choice + 1, :] == expert
        named = jnp.where(same, 1.0, named)
        chosen = jnp.where(same, raised, chosen)
        whole = whole + raised
    row = lax.broadcasted_iota(jnp.int32, (128, 128), 0)
    column = lax.broadcasted_iota(jnp.int32, (128, 128), 1)
    before = jnp.where(row < column, 1.0, 0.0).astype(BF16)
    rank = jnp.dot(named.astype(BF16), before, preferred_element_type=F32)
    weight = chosen / whole * RETURN_SCALE
    high = weight.astype(BF16).astype(F32)
    last = jnp.concatenate(
        [
            tokens_ref[1408:, :].astype(F32),
            jnp.where(named > 0.0, rank, 128.0),
            high,
            weight - high,
            jnp.zeros((48, 128), F32),
        ],
        axis=0,
    )
    out_ref[:, 1408:] = last.T.astype(BF16)


def pack(tokens, route_ids, route_level):
    return pl.pallas_call(
        pack_kernel,
        out_shape=jax.ShapeDtypeStruct((128, WIDE), BF16),
        compiler_params=pltpu.CompilerParams(vmem_limit_bytes=VMEM_LIMIT),
        name="pack",
    )(tokens.T, route_ids.T, route_level.T)


def relay(block, after):
    return lax.optimization_barrier((block, after))[0]


def combine_weights(shard_ref, place_ref):
    lane = lax.broadcasted_iota(jnp.int32, (128, 384), 1)
    source = lax.broadcasted_iota(jnp.int32, (128, 384), 0)
    expert = jnp.where(jnp.bitwise_and(lane, 127) < MOST, place_ref[0], place_ref[1])
    wanted = 32 + 16 * jnp.right_shift(lane, 7) + expert
    spread = jnp.where(source == wanted, 1.0, 0.0).astype(BF16)
    slot = jnp.bitwise_and(lane[:, :128], MOST - 1).astype(F32)
    meta = jnp.dot(shard_ref[:, 1408:1536], spread, preferred_element_type=F32)
    keep = meta[:, :128] == slot
    parts = [jnp.where(keep, meta[:, 128 * i : 128 * i + 128], 0.0) for i in (1, 2)]
    return jnp.concatenate(parts, axis=1).astype(BF16)


def expert_kernel(count, place_ref, *refs):
    shards = refs[:count]
    (
        first_ref,
        second_ref,
        first_bias_ref,
        second_bias_ref,
        mine_ref,
        other_ref,
        weight_ref,
        rows_ref,
        total_ref,
    ) = refs[count:]
    chunk = pl.program_id(0)
    half = count // 2 * MOST

    @pl.when(chunk == 0)
    def _():
        lane = lax.broadcasted_iota(jnp.int32, (128, 128), 1)
        source = lax.broadcasted_iota(jnp.int32, (128, 128), 0)
        spread = jnp.where(source == 32 + place_ref[0], 1.0, 0.0).astype(BF16)
        slot = jnp.bitwise_and(lane, MOST - 1).astype(F32)
        lower = lane < MOST
        for j in range(0, count, 2):
            picks = []
            for i in range(2):
                at = jnp.dot(shards[j + i][:, 1408:1536], spread, preferred_element_type=F32)
                keep = (at == slot) & (lower if i == 0 else jnp.logical_not(lower))
                picks.append(jnp.where(keep, 1.0, 0.0).astype(BF16))
                if j + i < count // 2:
                    weight_ref[j + i] = combine_weights(shards[j + i], place_ref)
            rows = lax.dot_general(
                jnp.concatenate(picks, axis=0),
                jnp.concatenate([shards[j][...], shards[j + 1][...]], axis=0),
                (((0,), (0,)), ((), ())),
                preferred_element_type=F32,
            )
            rows_ref[MOST * j : MOST * j + 2 * MOST, :] = rows.astype(BF16)

    pre = jnp.dot(rows_ref[:, :1440], first_ref[0], preferred_element_type=F32)
    pre = pre + first_bias_ref[chunk]
    gate = jnp.minimum(pre[:, :512], 7.0)
    up = jnp.clip(pre[:, 512:], -7.0, 7.0)
    activated = ((up + 1.0) * gate * (0.5 + 0.5 * jnp.tanh(0.851 * gate))).astype(BF16)
    product = jnp.dot(activated, second_ref[0], preferred_element_type=F32)

    @pl.when(chunk == 0)
    def _():
        total_ref[...] = product + second_bias_ref[...]

    @pl.when(chunk == 1)
    def _():
        total_ref[...] += product

    @pl.when(chunk == CHUNKS - 1)
    def _():
        done = (total_ref[...] + product).astype(BF16)
        mine_ref[...] = done[:half]
        other_ref[...] = done[half:]


def run_experts(shards, experts, first, second, first_bias, second_bias):
    count = len(shards)
    rows = count * MOST
    half = jax.ShapeDtypeStruct((rows // 2, WIDE), BF16)
    half_spec = pl.BlockSpec(memory_space=pltpu.VMEM)
    return pl.pallas_call(
        functools.partial(expert_kernel, count),
        grid_spec=pltpu.PrefetchScalarGridSpec(
            num_scalar_prefetch=1,
            grid=(CHUNKS,),
            in_specs=[pl.BlockSpec(memory_space=pltpu.VMEM)] * count
            + [
                pl.BlockSpec((1, 1440, 1024), lambda b, place: (b, 0, 0)),
                pl.BlockSpec((1, 512, WIDE), lambda b, place: (b, 0, 0)),
                pl.BlockSpec((CHUNKS, 1, 1024), lambda b, place: (0, 0, 0)),
                pl.BlockSpec((1, WIDE), lambda b, place: (0, 0)),
            ],
            out_specs=[half_spec] * 3,
            scratch_shapes=[pltpu.VMEM((rows, WIDE), BF16), pltpu.VMEM((rows, WIDE), F32)],
        ),
        out_shape=[half, half, jax.ShapeDtypeStruct((count // 2, 128, 256), BF16)],
        compiler_params=pltpu.CompilerParams(vmem_limit_bytes=VMEM_LIMIT),
        cost_estimate=pl.CostEstimate(
            flops=4 * rows * 1440 * 4320, bytes_accessed=30_000_000, transcendentals=0
        ),
        name="experts",
    )(experts, *shards, first, second, first_bias, second_bias)


def combine_kernel(count, weight_ref, mine_ref, other_ref, *outs):
    for j in range(count):
        mine = mine_ref[MOST * j : MOST * j + MOST, :]
        other = other_ref[MOST * j : MOST * j + MOST, :]
        outs[j][...] = jnp.dot(
            weight_ref[j],
            jnp.concatenate([mine, other, mine, other], axis=0),
            preferred_element_type=F32,
        )


def combine(weight, mine, other):
    count = weight.shape[0]
    return pl.pallas_call(
        functools.partial(combine_kernel, count),
        in_specs=[pl.BlockSpec(memory_space=pltpu.VMEM)] * 3,
        out_specs=[pl.BlockSpec(memory_space=pltpu.VMEM)] * count,
        out_shape=[jax.ShapeDtypeStruct((128, WIDE), F32)] * count,
        compiler_params=pltpu.CompilerParams(vmem_limit_bytes=SMALL_LIMIT),
        cost_estimate=pl.CostEstimate(
            flops=2 * count * 128 * 256 * WIDE, bytes_accessed=1_500_000 * count, transcendentals=0
        ),
        name="combine",
    )(weight, mine, other)


def turned(block, cosine, sine_part):
    width = block.shape[1]
    lane = lax.broadcasted_iota(jnp.int32, block.shape, 1)
    first = jnp.bitwise_and(lane, 63) < 32
    swapped = jnp.where(first, pltpu.roll(block, width - 32, 1), pltpu.roll(block, 32, 1))
    copies = width // 128
    cosine = jnp.concatenate([cosine] * copies, axis=1)
    sine_part = jnp.concatenate([sine_part] * copies, axis=1)
    return block * cosine + swapped * sine_part


def mix_kernel(
    tokens_ref, mixture_ref, gain_ref, key_ref, value_ref, cos_ref, sin_ref, out_ref, normed_ref, kv_ref
):
    block_out = (tokens_ref[:, :1440].astype(F32) + mixture_ref[...]).astype(BF16)
    out_ref[...] = block_out
    widened = block_out.astype(F32)
    squares = jnp.sum(widened * widened, axis=1, keepdims=True) / 1440.0
    normed = (widened * lax.rsqrt(squares + 1e-05) * gain_ref[...].astype(F32)).astype(BF16)
    normed_ref[...] = normed
    keys = jnp.dot(normed, key_ref[...], preferred_element_type=F32)
    kv_ref[:, :256] = turned(keys, cos_ref[...], sin_ref[...]).astype(BF16)
    kv_ref[:, 256:] = jnp.dot(normed, value_ref[...], preferred_element_type=F32).astype(BF16)


def mix(tokens, mixture, gain, key_matrix, value_matrix, cosine, sine_part):
    return pl.pallas_call(
        mix_kernel,
        out_shape=[
            jax.ShapeDtypeStruct((128, 1440), BF16),
            jax.ShapeDtypeStruct((128, 1440), BF16),
            jax.ShapeDtypeStruct((128, 512), BF16),
        ],
        compiler_params=pltpu.CompilerParams(vmem_limit_bytes=VMEM_LIMIT),
        cost_estimate=pl.CostEstimate(
            flops=2 * 128 * 1440 * 512, bytes_accessed=3_000_000, transcendentals=0
        ),
        name="mix",
    )(tokens, mixture, gain, key_matrix, value_matrix, cosine, sine_part)


def queries_kernel(normed_ref, weight_ref, cos_ref, sin_ref, out_ref):
    projected = jnp.dot(normed_ref[...], weight_ref[...], preferred_element_type=F32)
    rotated = turned(projected, cos_ref[...], sin_ref[...])
    scaled = (rotated.astype(BF16).astype(F32) * 0.125).astype(BF16)
    for pair in range(4):
        out_ref[0, 128 * pair : 128 * pair + 128, :] = scaled[:, 128 * pair : 128 * pair + 128]


def queries(normed, weight, cosine, sine_part):
    return pl.pallas_call(
        queries_kernel,
        grid=(4,),
        in_specs=[
            pl.BlockSpec((128, 1440), lambda g: (0, 0)),
            pl.BlockSpec((1440, 512), lambda g: (0, g)),
            pl.BlockSpec((128, 128), lambda g: (0, 0)),
            pl.BlockSpec((128, 128), lambda g: (0, 0)),
        ],
        out_specs=pl.BlockSpec((1, 512, 128), lambda g: (g, 0, 0)),
        out_shape=jax.ShapeDtypeStruct((4, 512, 128), BF16),
        compiler_params=pltpu.CompilerParams(vmem_limit_bytes=VMEM_LIMIT),
        cost_estimate=pl.CostEstimate(
            flops=2 * 128 * 1440 * 2048, bytes_accessed=7_000_000, transcendentals=0
        ),
        name="queries",
    )(normed, weight, cosine, sine_part)


def attend_kernel(index_ref, sinks_ref, queries_ref, own_ref, halo_ref, out_ref):
    lane = lax.broadcasted_iota(jnp.int32, (128, 128), 1)
    lower = lane < 64

    def doubled(block, odd):
        block = block.astype(F32)
        if odd:
            high = jnp.where(lower, 0.0, block)
            low = pltpu.roll(high, 64, 1)
        else:
            low = jnp.where(lower, block, 0.0)
            high = pltpu.roll(low, 64, 1)
        return jnp.concatenate([low, high], axis=0).astype(BF16)

    row = lax.broadcasted_iota(jnp.int32, (128, 256), 0)
    column = jnp.bitwise_and(lax.broadcasted_iota(jnp.int32, (128, 256), 1), 127)
    mine = column <= row
    allowed = mine | jnp.broadcast_to(index_ref[0] > 0, mine.shape)
    for group in range(4):
        start = 128 * (group // 2)
        odd = group % 2 == 1
        query = queries_ref[group]
        across = (((1,), (1,)), ((), ()))
        here = lax.dot_general(
            query, doubled(own_ref[:, start : start + 128], odd), across, preferred_element_type=F32
        )
        there = lax.dot_general(
            query, doubled(halo_ref[:, start : start + 128], odd), across, preferred_element_type=F32
        )
        here_probs = []
        there_probs = []
        for pair in range(4):
            rows = slice(128 * pair, 128 * pair + 128)
            scores = jnp.where(mine, here[rows], there[rows])
            scores = jnp.where(allowed, scores, -1e30)
            halves = []
            for side in range(2):
                part = scores[:, 128 * side : 128 * side + 128]
                sink = sinks_ref[8 * group + 2 * pair + side]
                top = jnp.maximum(jnp.max(part, axis=1, keepdims=True), sink)
                weights = jnp.exp(part - top)
                whole = jnp.exp(sink - top) + jnp.sum(weights, axis=1, keepdims=True)
                halves.append(weights * (1.0 / whole))
            probs = jnp.where(allowed, jnp.concatenate(halves, axis=1), 0.0)
            here_probs.append(jnp.where(mine, probs, 0.0).astype(BF16))
            there_probs.append(jnp.where(mine, 0.0, probs).astype(BF16))
        mixed = jnp.dot(
            jnp.concatenate(here_probs, axis=0),
            doubled(own_ref[:, 256 + start : 384 + start], odd),
            preferred_element_type=F32,
        ) + jnp.dot(
            jnp.concatenate(there_probs, axis=0),
            doubled(halo_ref[:, 256 + start : 384 + start], odd),
            preferred_element_type=F32,
        )
        for pair in range(4):
            place = 512 * group + 128 * pair
            out_ref[:, place : place + 128] = mixed[128 * pair : 128 * pair + 128].astype(BF16)


def attend(index, sinks, query, own, halo):
    return pl.pallas_call(
        attend_kernel,
        in_specs=[
            pl.BlockSpec(memory_space=pltpu.SMEM),
            pl.BlockSpec(memory_space=pltpu.SMEM),
            pl.BlockSpec(memory_space=pltpu.VMEM),
            pl.BlockSpec(memory_space=pltpu.VMEM),
            pl.BlockSpec(memory_space=pltpu.VMEM),
        ],
        out_specs=pl.BlockSpec(memory_space=pltpu.VMEM),
        out_shape=jax.ShapeDtypeStruct((128, 2048), BF16),
        compiler_params=pltpu.CompilerParams(vmem_limit_bytes=VMEM_LIMIT),
        cost_estimate=pl.CostEstimate(
            flops=2 * 32 * 128 * 256 * 128, bytes_accessed=1_500_000, transcendentals=1_000_000
        ),
        name="attend",
    )(index, sinks, query, own, halo)


def body(
    tokens,
    route_ids,
    route_level,
    gate_up_codes,
    gate_up_scale,
    gate_up_bias,
    down_codes,
    down_scale,
    down_bias,
    attn_gain,
    query_weight,
    key_matrix,
    value_matrix,
    sinks,
):
    own_tokens, width = tokens.shape
    group_size = lax.axis_size("expert")
    far = group_size // 4
    device_index = lax.axis_index("expert")
    core = device_index % 2

    partner = [(i, i ^ 1) for i in range(group_size)]

    def swap(block):
        return lax.ppermute(block, "expert", partner)

    def inward(block, across):
        route = []
        for i in range(group_size):
            goal = (i + (-2 if i % 2 else 2)) % group_size
            route.append((i ^ 1 if across else i, goal))
        return lax.ppermute(block, "expert", route)

    packed = pack(tokens, route_ids, route_level)

    second = decode_down(down_codes[0], down_scale[0])
    first, first_bias = decode_up(gate_up_codes[0], gate_up_scale[0], gate_up_bias)
    second_bias = jnp.pad(down_bias.astype(F32), ((0, 0), (0, WIDE - width)))
    experts = jnp.stack([device_index, device_index + 1 - 2 * core]).astype(jnp.int32)

    def serve(blocks, after):
        return run_experts(
            blocks + [swap(block) for block in blocks],
            relay(experts, after),
            first,
            second,
            first_bias,
            second_bias,
        )

    def gather(served):
        rows, given, weight = served
        return combine(weight, rows, swap(given))

    same = [packed, inward(packed, False)]
    cross = [packed, inward(packed, True)]
    same[1] = relay(same[1], second)
    same.append(inward(same[1], False))
    cross.append(inward(cross[1], False))
    same[2] = relay(same[2], first)
    same.append(inward(same[2], False))
    cross.append(inward(cross[2], False))
    served_near = serve([same[1], cross[1], packed], packed)
    same[3] = relay(same[3], served_near)
    same.append(inward(same[3], False))
    served_middle = serve([same[2], cross[2]], served_near)
    same[far] = relay(same[far], served_middle)
    served_far = serve([same[far], same[far - 1], cross[far - 1]], served_middle)
    same_far, same_third, cross_third = gather(served_far)
    same_near = [None, None, None]
    cross_near = [None, None, None]
    same_near[2], cross_near[2] = gather(relay(served_middle, same_far))
    same_near[1], cross_near[1], own = gather(relay(served_near, same_far))

    half_dim = HEAD_SIZE // 2
    frequency = jnp.power(
        jnp.float32(150000.0), -2.0 * jnp.arange(half_dim, dtype=F32) / (2 * half_dim)
    )
    token_positions = device_index * own_tokens + jnp.arange(own_tokens, dtype=jnp.int32)
    angles = token_positions.astype(F32)[:, None] * frequency[None, :]
    cosine = jnp.tile(jnp.cos(angles), (1, 4))
    sine_part = jnp.sin(angles)
    sine_part = jnp.concatenate([-sine_part, sine_part, -sine_part, sine_part], axis=1)

    def onward(block, across):
        route = []
        for i in range(group_size):
            goal = (i + (2 if i % 2 else -2)) % group_size
            route.append((i, goal ^ 1 if across else goal))
        return lax.ppermute(block.astype(jnp.float16), "expert", route).astype(F32)

    from_same = onward(same_far, False)
    from_cross = onward(cross_third, False)
    from_same = onward(same_third + from_same, False)
    from_same = onward(same_near[2] + from_same, False)
    from_cross = onward(cross_near[2] + from_cross, False)
    from_same = onward(same_near[1] + from_same, False)
    from_cross = onward(cross_near[1] + from_cross, True)
    mixture = (own + from_same + from_cross)[:, :width] * (1.0 / RETURN_SCALE)

    block_out, normed, own_kv = mix(
        packed, mixture, attn_gain[None], key_matrix, value_matrix, cosine, sine_part
    )
    ahead = [(i, i + 1) for i in range(group_size - 1)]
    halo_kv = lax.ppermute(own_kv, "expert", ahead)
    query = queries(normed, query_weight, cosine, sine_part)
    attended = attend(device_index.reshape(1), sinks, query, own_kv, halo_kv)
    return (block_out, attended)


def solution(mesh):
    in_specs = (
        P(("dp", "expert"), None),
        P(("dp", "expert"), None),
        P(("dp", "expert"), None),
        P("expert", None, None),
        P("expert", None, None),
        P("expert", None),
        P("expert", None, None),
        P("expert", None, None),
        P("expert", None),
        P(),
        P(),
        P(),
        P(),
        P(),
    )
    out_specs = (P(("dp", "expert"), None), P(("dp", "expert"), None))
    return jax.shard_map(body, mesh=mesh, in_specs=in_specs, out_specs=out_specs, check_vma=False)
```

```python
import functools

import jax
import jax.numpy as jnp
from jax import lax
from jax.experimental import pallas as pl
from jax.experimental.pallas import tpu as pltpu
from jax.sharding import PartitionSpec as P

HEAD_SIZE = 64
WINDOW_LENGTH = 128
MOST = 64
WIDE = 1536
CHUNKS = 3
RETURN_SCALE = 8.0
LARGE_LIMIT = 56 * 1024 * 1024
VMEM_LIMIT = 22 * 1024 * 1024
SMALL_LIMIT = 16 * 1024 * 1024
F32 = jnp.float32
BF16 = jnp.bfloat16


def twice_fp4(words, field_index):
    field = jnp.bitwise_and(jnp.right_shift(words, 4 * field_index), 15).astype(F32).astype(BF16)
    negative = field >= 8
    low = jnp.where(negative, field - 8, field)
    return negative, jnp.maximum(jnp.maximum(low, 2 * low - 4), 4 * low - 16)


def power_of_two(exponents, least, valid):
    step = exponents - least
    scale = jnp.where(step == 0, 1.0, jnp.where(step == 1, 2.0, jnp.where(step == 2, 4.0, 8.0)))
    return jnp.where(valid, scale * 2.0 ** (least - 128), 0.0)


def decode_up_kernel(codes_ref, exponent_ref, bias_ref, out_ref, bias_out_ref, scale_ref):
    chunk = pl.program_id(0)
    source = lax.broadcasted_iota(jnp.int32, (512, 512), 0)
    target = lax.broadcasted_iota(jnp.int32, (512, 512), 1)
    wanted = 128 * jnp.bitwise_and(source, 3) + jnp.right_shift(source, 2)
    spread = jnp.where(target == wanted, 1.0, 0.0).astype(BF16)
    for half in range(2):
        lanes = slice(512 * half, 512 * half + 512)
        left = 2880 - 1024 * chunk - 512 * half
        column = lax.broadcasted_iota(jnp.int32, (45, 512), 1)
        scale = power_of_two(exponent_ref[:, lanes], 119, column < left)
        scale = jnp.dot(scale.astype(BF16), spread, preferred_element_type=F32)
        bias = jnp.where(column[:1] < left, bias_ref[:, lanes].astype(F32), 0.0)
        bias = jnp.broadcast_to(bias, (16, 512)).astype(BF16)
        bias = jnp.dot(bias, spread, preferred_element_type=F32)
        for place, field_index in enumerate((0, 2, 1, 3)):
            taken = slice(128 * field_index, 128 * field_index + 128)
            given = slice(256 * place + 128 * half, 256 * place + 128 * half + 128)
            scale_ref[:45, given] = scale[:, taken]
            bias_out_ref[0, :, given] = bias[:1, taken]
    for block in range(45):
        words = codes_ref[32 * block : 32 * block + 32, :]
        for place, field_index in enumerate((0, 2, 1, 3)):
            lanes = slice(256 * place, 256 * place + 256)
            scale = scale_ref[block : block + 1, lanes]
            negative, size = twice_fp4(words, field_index)
            scale = jnp.broadcast_to(scale.astype(BF16), size.shape)
            out_ref[0, 32 * block : 32 * block + 32, lanes] = size * jnp.where(
                negative, -scale, scale
            )


def decode_up(codes, exponents, bias):
    rows = codes.shape[0]
    return pl.pallas_call(
        decode_up_kernel,
        grid=(CHUNKS,),
        in_specs=[
            pl.BlockSpec((1440, 256), lambda b: (0, b)),
            pl.BlockSpec((45, 1024), lambda b: (0, b)),
            pl.BlockSpec((1, 1024), lambda b: (0, b)),
        ],
        out_specs=[
            pl.BlockSpec((1, 1440, 1024), lambda b: (b, 0, 0)),
            pl.BlockSpec((1, 1, 1024), lambda b: (b, 0, 0)),
        ],
        out_shape=[
            jax.ShapeDtypeStruct((CHUNKS, rows, 1024), BF16),
            jax.ShapeDtypeStruct((CHUNKS, 1, 1024), F32),
        ],
        scratch_shapes=[pltpu.VMEM((48, 1024), F32)],
        compiler_params=pltpu.CompilerParams(vmem_limit_bytes=LARGE_LIMIT),
        cost_estimate=pl.CostEstimate(flops=60_000_000, bytes_accessed=30_000_000, transcendentals=0),
        name="decode_up",
    )(codes, exponents, bias)


def decode_down_kernel(
    left_ref, middle_ref, right_ref, left_exp_ref, middle_exp_ref, right_exp_ref, out_ref
):
    row = lax.broadcasted_iota(jnp.int32, (16, 512), 0) + 16 * pl.program_id(0)
    column = lax.broadcasted_iota(jnp.int32, (16, 512), 1)
    scales = [
        power_of_two(exponent_ref[...], 117, (row < 45) & (column < 1440 - 512 * part))
        for part, exponent_ref in enumerate((left_exp_ref, middle_exp_ref, right_exp_ref))
    ]
    source = lax.broadcasted_iota(jnp.int32, (512, 512), 0)
    target = lax.broadcasted_iota(jnp.int32, (512, 512), 1)
    wanted = 4 * jnp.bitwise_and(source, 127) + jnp.right_shift(source, 7)
    spread = jnp.where(target == wanted, 1.0, 0.0).astype(BF16)
    for parity in range(2):
        for part, codes_ref in enumerate((left_ref, middle_ref, right_ref)):
            piece = codes_ref[pl.ds(parity, 256, 2), :]
            fields = []
            for field_index in range(4):
                negative, size = twice_fp4(piece, field_index)
                fields.append(jnp.where(negative, -size, size))
            natural = jnp.dot(
                jnp.concatenate(fields, axis=1), spread, preferred_element_type=F32
            )
            for block in range(16):
                scale = scales[part][block : block + 1, :]
                row = 256 * parity + 16 * block
                out_ref[pl.program_id(0), row : row + 16, 512 * part : 512 * part + 512] = (
                    natural[16 * block : 16 * block + 16] * scale
                ).astype(BF16)


def decode_down(codes, exponents):
    return pl.pallas_call(
        decode_down_kernel,
        grid=(CHUNKS,),
        in_specs=[
            pl.BlockSpec((512, 128), lambda b: (b, 0)),
            pl.BlockSpec((512, 128), lambda b: (b, 1)),
            pl.BlockSpec((512, 128), lambda b: (b, 2)),
            pl.BlockSpec((16, 512), lambda b: (b, 0)),
            pl.BlockSpec((16, 512), lambda b: (b, 1)),
            pl.BlockSpec((16, 512), lambda b: (b, 2)),
        ],
        out_specs=pl.BlockSpec(memory_space=pltpu.VMEM),
        out_shape=jax.ShapeDtypeStruct((CHUNKS, 512, WIDE), BF16),
        compiler_params=pltpu.CompilerParams(vmem_limit_bytes=SMALL_LIMIT),
        cost_estimate=pl.CostEstimate(flops=60_000_000, bytes_accessed=20_000_000, transcendentals=0),
        name="decode_down",
    )(codes, codes, codes, exponents, exponents, exponents)


def pack_kernel(tokens_ref, ids_ref, level_ref, out_ref):
    for place in range(11):
        block = tokens_ref[128 * place : 128 * place + 128, :].astype(F32)
        out_ref[:, 128 * place : 128 * place + 128] = block.T.astype(BF16)
    expert = lax.broadcasted_iota(jnp.int32, (16, 128), 0)
    named = jnp.zeros((16, 128), F32)
    chosen = jnp.zeros((16, 128), F32)
    whole = jnp.zeros((1, 128), F32)
    for choice in range(4):
        raised = jnp.exp(level_ref[choice : choice + 1, :].astype(F32) / 4.0)
        same = ids_ref[choice : choice + 1, :] == expert
        named = jnp.where(same, 1.0, named)
        chosen = jnp.where(same, raised, chosen)
        whole = whole + raised
    row = lax.broadcasted_iota(jnp.int32, (128, 128), 0)
    column = lax.broadcasted_iota(jnp.int32, (128, 128), 1)
    before = jnp.where(row < column, 1.0, 0.0).astype(BF16)
    rank = jnp.dot(named.astype(BF16), before, preferred_element_type=F32)
    weight = chosen / whole * RETURN_SCALE
    high = weight.astype(BF16).astype(F32)
    last = jnp.concatenate(
        [
            tokens_ref[1408:, :].astype(F32),
            jnp.where(named > 0.0, rank, 128.0),
            high,
            weight - high,
            jnp.zeros((48, 128), F32),
        ],
        axis=0,
    )
    out_ref[:, 1408:] = last.T.astype(BF16)


def pack(tokens, route_ids, route_level):
    return pl.pallas_call(
        pack_kernel,
        grid=(1,),
        in_specs=[
            pl.BlockSpec((1440, 128), lambda i: (0, 0)),
            pl.BlockSpec((4, 128), lambda i: (0, 0)),
            pl.BlockSpec((4, 128), lambda i: (0, 0)),
        ],
        out_specs=pl.BlockSpec(memory_space=pltpu.VMEM),
        out_shape=jax.ShapeDtypeStruct((128, WIDE), BF16),
        compiler_params=pltpu.CompilerParams(vmem_limit_bytes=LARGE_LIMIT),
        name="pack",
    )(tokens.T, route_ids.T, route_level.T)


def relay(block, after):
    return lax.optimization_barrier((block, after))[0]


def combine_weights(shard_ref, place_ref):
    lane = lax.broadcasted_iota(jnp.int32, (128, 384), 1)
    source = lax.broadcasted_iota(jnp.int32, (128, 384), 0)
    expert = jnp.where(jnp.bitwise_and(lane, 127) < MOST, place_ref[0], place_ref[1])
    wanted = 32 + 16 * jnp.right_shift(lane, 7) + expert
    spread = jnp.where(source == wanted, 1.0, 0.0).astype(BF16)
    slot = jnp.bitwise_and(lane[:, :128], MOST - 1).astype(F32)
    meta = jnp.dot(shard_ref[:, 1408:1536], spread, preferred_element_type=F32)
    keep = meta[:, :128] == slot
    parts = [jnp.where(keep, meta[:, 128 * i : 128 * i + 128], 0.0) for i in (1, 2)]
    return jnp.concatenate(parts, axis=1).astype(BF16)


def expert_kernel(count, place_ref, *refs):
    shards = refs[:count]
    (
        first_ref,
        second_ref,
        first_bias_ref,
        second_bias_ref,
        mine_ref,
        other_ref,
        weight_ref,
        rows_ref,
        total_ref,
    ) = refs[count:]
    chunk = pl.program_id(0)
    half = count // 2 * MOST

    @pl.when(chunk == 0)
    def _():
        lane = lax.broadcasted_iota(jnp.int32, (128, 128), 1)
        source = lax.broadcasted_iota(jnp.int32, (128, 128), 0)
        spread = jnp.where(source == 32 + place_ref[0], 1.0, 0.0).astype(BF16)
        slot = jnp.bitwise_and(lane, MOST - 1).astype(F32)
        lower = lane < MOST
        for j in range(0, count, 2):
            picks = []
            for i in range(2):
                at = jnp.dot(shards[j + i][:, 1408:1536], spread, preferred_element_type=F32)
                keep = (at == slot) & (lower if i == 0 else jnp.logical_not(lower))
                picks.append(jnp.where(keep, 1.0, 0.0).astype(BF16))
                if j + i < count // 2:
                    weight_ref[j + i] = combine_weights(shards[j + i], place_ref)
            rows = lax.dot_general(
                jnp.concatenate(picks, axis=0),
                jnp.concatenate([shards[j][...], shards[j + 1][...]], axis=0),
                (((0,), (0,)), ((), ())),
                preferred_element_type=F32,
            )
            rows_ref[MOST * j : MOST * j + 2 * MOST, :] = rows.astype(BF16)

    rows = rows_ref[:, :1440]
    activated = []
    for part in range(2):
        pre = []
        for start in (256 * part, 512 + 256 * part):
            lanes = slice(start, start + 256)
            pre.append(
                jnp.dot(rows, first_ref[chunk, :, lanes], preferred_element_type=F32)
                + first_bias_ref[chunk, :, lanes]
            )
        gate = jnp.minimum(pre[0], 7.0)
        up = jnp.clip(pre[1], -7.0, 7.0)
        activated.append(
            ((up + 1.0) * gate * (0.5 + 0.5 * jnp.tanh(0.851 * gate))).astype(BF16)
        )
    product = jnp.dot(
        jnp.concatenate(activated, axis=1), second_ref[chunk], preferred_element_type=F32
    )

    @pl.when(chunk == 0)
    def _():
        total_ref[...] = product + second_bias_ref[...]

    @pl.when(chunk == 1)
    def _():
        total_ref[...] += product

    @pl.when(chunk == CHUNKS - 1)
    def _():
        done = (total_ref[...] + product).astype(BF16)
        mine_ref[...] = done[:half]
        other_ref[...] = done[half:]


def run_experts(shards, experts, first, second, first_bias, second_bias):
    count = len(shards)
    rows = count * MOST
    half = jax.ShapeDtypeStruct((rows // 2, WIDE), BF16)
    half_spec = pl.BlockSpec(memory_space=pltpu.VMEM)
    return pl.pallas_call(
        functools.partial(expert_kernel, count),
        grid_spec=pltpu.PrefetchScalarGridSpec(
            num_scalar_prefetch=1,
            grid=(CHUNKS,),
            in_specs=[pl.BlockSpec(memory_space=pltpu.VMEM)] * count
            + [
                pl.BlockSpec(memory_space=pltpu.VMEM),
                pl.BlockSpec(memory_space=pltpu.VMEM),
                pl.BlockSpec((CHUNKS, 1, 1024), lambda b, place: (0, 0, 0)),
                pl.BlockSpec((1, WIDE), lambda b, place: (0, 0)),
            ],
            out_specs=[half_spec] * 3,
            scratch_shapes=[pltpu.VMEM((rows, WIDE), BF16), pltpu.VMEM((rows, WIDE), F32)],
        ),
        out_shape=[half, half, jax.ShapeDtypeStruct((count // 2, 128, 256), BF16)],
        compiler_params=pltpu.CompilerParams(vmem_limit_bytes=VMEM_LIMIT),
        cost_estimate=pl.CostEstimate(
            flops=4 * rows * 1440 * 4320, bytes_accessed=30_000_000, transcendentals=0
        ),
        name="experts",
    )(experts, *shards, first, second, first_bias, second_bias)


def combine_kernel(count, weight_ref, mine_ref, other_ref, *outs):
    for j in range(count):
        mine = mine_ref[MOST * j : MOST * j + MOST, :]
        other = other_ref[MOST * j : MOST * j + MOST, :]
        outs[j][...] = jnp.dot(
            weight_ref[j],
            jnp.concatenate([mine, other, mine, other], axis=0),
            preferred_element_type=F32,
        )


def combine(weight, mine, other):
    count = weight.shape[0]
    return pl.pallas_call(
        functools.partial(combine_kernel, count),
        in_specs=[pl.BlockSpec(memory_space=pltpu.VMEM)] * 3,
        out_specs=[pl.BlockSpec(memory_space=pltpu.VMEM)] * count,
        out_shape=[jax.ShapeDtypeStruct((128, WIDE), F32)] * count,
        compiler_params=pltpu.CompilerParams(vmem_limit_bytes=SMALL_LIMIT),
        cost_estimate=pl.CostEstimate(
            flops=2 * count * 128 * 256 * WIDE, bytes_accessed=1_500_000 * count, transcendentals=0
        ),
        name="combine",
    )(weight, mine, other)


def turned(block, cosine, sine_part):
    width = block.shape[1]
    lane = lax.broadcasted_iota(jnp.int32, block.shape, 1)
    first = jnp.bitwise_and(lane, 63) < 32
    swapped = jnp.where(first, pltpu.roll(block, width - 32, 1), pltpu.roll(block, 32, 1))
    copies = width // 128
    cosine = jnp.concatenate([cosine] * copies, axis=1)
    sine_part = jnp.concatenate([sine_part] * copies, axis=1)
    return block * cosine + swapped * sine_part


def mix_kernel(
    tokens_ref, mixture_ref, gain_ref, key_ref, value_ref, cos_ref, sin_ref, out_ref, normed_ref, kv_ref
):
    block_out = (tokens_ref[:, :1440].astype(F32) + mixture_ref[...]).astype(BF16)
    out_ref[...] = block_out
    widened = block_out.astype(F32)
    squares = jnp.sum(widened * widened, axis=1, keepdims=True) / 1440.0
    normed = (widened * lax.rsqrt(squares + 1e-05) * gain_ref[...].astype(F32)).astype(BF16)
    normed_ref[...] = normed
    keys = jnp.dot(normed, key_ref[...], preferred_element_type=F32)
    kv_ref[:, :256] = turned(keys, cos_ref[...], sin_ref[...]).astype(BF16)
    kv_ref[:, 256:] = jnp.dot(normed, value_ref[...], preferred_element_type=F32).astype(BF16)


def mix(tokens, mixture, gain, key_matrix, value_matrix, cosine, sine_part):
    return pl.pallas_call(
        mix_kernel,
        out_shape=[
            jax.ShapeDtypeStruct((128, 1440), BF16),
            jax.ShapeDtypeStruct((128, 1440), BF16),
            jax.ShapeDtypeStruct((128, 512), BF16),
        ],
        compiler_params=pltpu.CompilerParams(vmem_limit_bytes=SMALL_LIMIT),
        cost_estimate=pl.CostEstimate(
            flops=2 * 128 * 1440 * 512, bytes_accessed=3_000_000, transcendentals=0
        ),
        name="mix",
    )(tokens, mixture, gain, key_matrix, value_matrix, cosine, sine_part)


def queries_kernel(normed_ref, weight_ref, cos_ref, sin_ref, out_ref):
    projected = jnp.dot(normed_ref[...], weight_ref[...], preferred_element_type=F32)
    rotated = turned(projected, cos_ref[...], sin_ref[...])
    scaled = (rotated.astype(BF16).astype(F32) * 0.125).astype(BF16)
    for pair in range(4):
        out_ref[0, 128 * pair : 128 * pair + 128, :] = scaled[:, 128 * pair : 128 * pair + 128]


def queries(normed, weight, cosine, sine_part):
    return pl.pallas_call(
        queries_kernel,
        grid=(4,),
        in_specs=[
            pl.BlockSpec((128, 1440), lambda g: (0, 0)),
            pl.BlockSpec((1440, 512), lambda g: (0, g)),
            pl.BlockSpec((128, 128), lambda g: (0, 0)),
            pl.BlockSpec((128, 128), lambda g: (0, 0)),
        ],
        out_specs=pl.BlockSpec((1, 512, 128), lambda g: (g, 0, 0)),
        out_shape=jax.ShapeDtypeStruct((4, 512, 128), BF16),
        compiler_params=pltpu.CompilerParams(vmem_limit_bytes=SMALL_LIMIT),
        cost_estimate=pl.CostEstimate(
            flops=2 * 128 * 1440 * 2048, bytes_accessed=7_000_000, transcendentals=0
        ),
        name="queries",
    )(normed, weight, cosine, sine_part)


def attend_kernel(index_ref, sinks_ref, queries_ref, own_ref, halo_ref, out_ref):
    lane = lax.broadcasted_iota(jnp.int32, (128, 128), 1)
    lower = lane < 64

    def doubled(block, odd):
        block = block.astype(F32)
        if odd:
            high = jnp.where(lower, 0.0, block)
            low = pltpu.roll(high, 64, 1)
        else:
            low = jnp.where(lower, block, 0.0)
            high = pltpu.roll(low, 64, 1)
        return jnp.concatenate([low, high], axis=0).astype(BF16)

    row = lax.broadcasted_iota(jnp.int32, (128, 256), 0)
    column = jnp.bitwise_and(lax.broadcasted_iota(jnp.int32, (128, 256), 1), 127)
    mine = column <= row
    allowed = mine | jnp.broadcast_to(index_ref[0] > 0, mine.shape)
    for group in range(4):
        start = 128 * (group // 2)
        odd = group % 2 == 1
        query = queries_ref[group]
        across = (((1,), (1,)), ((), ()))
        here = lax.dot_general(
            query, doubled(own_ref[:, start : start + 128], odd), across, preferred_element_type=F32
        )
        there = lax.dot_general(
            query, doubled(halo_ref[:, start : start + 128], odd), across, preferred_element_type=F32
        )
        here_probs = []
        there_probs = []
        for pair in range(4):
            rows = slice(128 * pair, 128 * pair + 128)
            scores = jnp.where(mine, here[rows], there[rows])
            scores = jnp.where(allowed, scores, -1e30)
            halves = []
            for side in range(2):
                part = scores[:, 128 * side : 128 * side + 128]
                sink = sinks_ref[8 * group + 2 * pair + side]
                top = jnp.maximum(jnp.max(part, axis=1, keepdims=True), sink)
                weights = jnp.exp(part - top)
                whole = jnp.exp(sink - top) + jnp.sum(weights, axis=1, keepdims=True)
                halves.append(weights * (1.0 / whole))
            probs = jnp.where(allowed, jnp.concatenate(halves, axis=1), 0.0)
            here_probs.append(jnp.where(mine, probs, 0.0).astype(BF16))
            there_probs.append(jnp.where(mine, 0.0, probs).astype(BF16))
        mixed = jnp.dot(
            jnp.concatenate(here_probs, axis=0),
            doubled(own_ref[:, 256 + start : 384 + start], odd),
            preferred_element_type=F32,
        ) + jnp.dot(
            jnp.concatenate(there_probs, axis=0),
            doubled(halo_ref[:, 256 + start : 384 + start], odd),
            preferred_element_type=F32,
        )
        for pair in range(4):
            place = 512 * group + 128 * pair
            out_ref[:, place : place + 128] = mixed[128 * pair : 128 * pair + 128].astype(BF16)


def attend(index, sinks, query, own, halo):
    return pl.pallas_call(
        attend_kernel,
        in_specs=[
            pl.BlockSpec(memory_space=pltpu.SMEM),
            pl.BlockSpec(memory_space=pltpu.SMEM),
            pl.BlockSpec(memory_space=pltpu.VMEM),
            pl.BlockSpec(memory_space=pltpu.VMEM),
            pl.BlockSpec(memory_space=pltpu.VMEM),
        ],
        out_specs=pl.BlockSpec(memory_space=pltpu.VMEM),
        out_shape=jax.ShapeDtypeStruct((128, 2048), BF16),
        compiler_params=pltpu.CompilerParams(vmem_limit_bytes=SMALL_LIMIT),
        cost_estimate=pl.CostEstimate(
            flops=2 * 32 * 128 * 256 * 128, bytes_accessed=1_500_000, transcendentals=1_000_000
        ),
        name="attend",
    )(index, sinks, query, own, halo)


def body(
    tokens,
    route_ids,
    route_level,
    gate_up_codes,
    gate_up_scale,
    gate_up_bias,
    down_codes,
    down_scale,
    down_bias,
    attn_gain,
    query_weight,
    key_matrix,
    value_matrix,
    sinks,
):
    own_tokens, width = tokens.shape
    group_size = lax.axis_size("expert")
    far = group_size // 4
    device_index = lax.axis_index("expert")
    core = device_index % 2

    partner = [(i, i ^ 1) for i in range(group_size)]

    def swap(block):
        return lax.ppermute(block, "expert", partner)

    def inward(block, across):
        route = []
        for i in range(group_size):
            goal = (i + (-2 if i % 2 else 2)) % group_size
            route.append((i ^ 1 if across else i, goal))
        return lax.ppermute(block, "expert", route)

    packed = pack(tokens, route_ids, route_level)

    second = decode_down(down_codes[0], down_scale[0])
    first, first_bias = decode_up(gate_up_codes[0], gate_up_scale[0], gate_up_bias)
    second_bias = jnp.pad(down_bias.astype(F32), ((0, 0), (0, WIDE - width)))
    experts = jnp.stack([device_index, device_index + 1 - 2 * core]).astype(jnp.int32)

    def serve(blocks, after):
        return run_experts(
            blocks + [swap(block) for block in blocks],
            relay(experts, after),
            first,
            second,
            first_bias,
            second_bias,
        )

    def gather(served):
        rows, given, weight = served
        return combine(weight, rows, swap(given))

    same = [packed, inward(packed, False)]
    cross = [packed, inward(packed, True)]
    same[1] = relay(same[1], first)
    same.append(inward(same[1], False))
    cross.append(inward(cross[1], False))
    same[2] = relay(same[2], second)
    same.append(inward(same[2], False))
    cross.append(inward(cross[2], False))
    served_near = serve([same[1], cross[1], packed], packed)
    same[3] = relay(same[3], served_near)
    same.append(inward(same[3], False))
    served_middle = serve([same[2], cross[2]], served_near)
    same[far] = relay(same[far], served_middle)
    served_far = serve([same[far], same[far - 1], cross[far - 1]], served_middle)
    same_far, same_third, cross_third = gather(served_far)
    same_near = [None, None, None]
    cross_near = [None, None, None]
    same_near[2], cross_near[2] = gather(relay(served_middle, same_far))
    same_near[1], cross_near[1], own = gather(relay(served_near, same_far))

    half_dim = HEAD_SIZE // 2
    frequency = jnp.power(
        jnp.float32(150000.0), -2.0 * jnp.arange(half_dim, dtype=F32) / (2 * half_dim)
    )
    token_positions = device_index * own_tokens + jnp.arange(own_tokens, dtype=jnp.int32)
    angles = token_positions.astype(F32)[:, None] * frequency[None, :]
    cosine = jnp.tile(jnp.cos(angles), (1, 4))
    sine_part = jnp.sin(angles)
    sine_part = jnp.concatenate([-sine_part, sine_part, -sine_part, sine_part], axis=1)

    def onward(block, across):
        route = []
        for i in range(group_size):
            goal = (i + (2 if i % 2 else -2)) % group_size
            route.append((i, goal ^ 1 if across else goal))
        return lax.ppermute(block.astype(jnp.float16), "expert", route).astype(F32)

    from_same = onward(same_far, False)
    from_cross = onward(cross_third, False)
    from_same = onward(same_third + from_same, False)
    from_same = onward(same_near[2] + from_same, False)
    from_cross = onward(cross_near[2] + from_cross, False)
    from_same = onward(same_near[1] + from_same, False)
    from_cross = onward(cross_near[1] + from_cross, True)
    mixture = (own + from_same + from_cross)[:, :width] * (1.0 / RETURN_SCALE)

    block_out, normed, own_kv = mix(
        packed, mixture, attn_gain[None], key_matrix, value_matrix, cosine, sine_part
    )
    ahead = [(i, i + 1) for i in range(group_size - 1)]
    halo_kv = lax.ppermute(own_kv, "expert", ahead)
    query = queries(normed, query_weight, cosine, sine_part)
    attended = attend(device_index.reshape(1), sinks, query, own_kv, halo_kv)
    return (block_out, attended)


def solution(mesh):
    in_specs = (
        P(("dp", "expert"), None),
        P(("dp", "expert"), None),
        P(("dp", "expert"), None),
        P("expert", None, None),
        P("expert", None, None),
        P("expert", None),
        P("expert", None, None),
        P("expert", None, None),
        P("expert", None),
        P(),
        P(),
        P(),
        P(),
        P(),
    )
    out_specs = (P(("dp", "expert"), None), P(("dp", "expert"), None))
    return jax.shard_map(body, mesh=mesh, in_specs=in_specs, out_specs=out_specs, check_vma=False)
```

```python
import functools

import jax
import jax.numpy as jnp
from jax import lax
from jax.experimental import pallas as pl
from jax.experimental.pallas import tpu as pltpu
from jax.sharding import PartitionSpec as P

HEAD_SIZE = 64
WINDOW_LENGTH = 128
MOST = 64
WIDE = 1536
CHUNKS = 3
RETURN_SCALE = 8.0
LARGE_LIMIT = 56 * 1024 * 1024
VMEM_LIMIT = 22 * 1024 * 1024
SMALL_LIMIT = 16 * 1024 * 1024
F32 = jnp.float32
BF16 = jnp.bfloat16


def twice_fp4(words, field_index):
    field = jnp.bitwise_and(jnp.right_shift(words, 4 * field_index), 15).astype(F32).astype(BF16)
    negative = field >= 8
    low = jnp.where(negative, field - 8, field)
    return negative, jnp.maximum(jnp.maximum(low, 2 * low - 4), 4 * low - 16)


def power_of_two(exponents, least, valid):
    step = exponents - least
    scale = jnp.where(step == 0, 1.0, jnp.where(step == 1, 2.0, jnp.where(step == 2, 4.0, 8.0)))
    return jnp.where(valid, scale * 2.0 ** (least - 128), 0.0)


def decode_up_kernel(codes_ref, exponent_ref, bias_ref, out_ref, bias_out_ref, scale_ref):
    chunk = pl.program_id(0)
    source = lax.broadcasted_iota(jnp.int32, (512, 512), 0)
    target = lax.broadcasted_iota(jnp.int32, (512, 512), 1)
    wanted = 128 * jnp.bitwise_and(source, 3) + jnp.right_shift(source, 2)
    spread = jnp.where(target == wanted, 1.0, 0.0).astype(BF16)
    for half in range(2):
        lanes = slice(512 * half, 512 * half + 512)
        left = 2880 - 1024 * chunk - 512 * half
        column = lax.broadcasted_iota(jnp.int32, (45, 512), 1)
        scale = power_of_two(exponent_ref[:, 0, lanes], 119, column < left)
        scale = jnp.dot(scale.astype(BF16), spread, preferred_element_type=F32)
        bias = jnp.where(column[:1] < left, bias_ref[:, lanes].astype(F32), 0.0)
        bias = jnp.broadcast_to(bias, (16, 512)).astype(BF16)
        bias = jnp.dot(bias, spread, preferred_element_type=F32)
        for place, field_index in enumerate((0, 2, 1, 3)):
            taken = slice(128 * field_index, 128 * field_index + 128)
            given = slice(256 * place + 128 * half, 256 * place + 128 * half + 128)
            scale_ref[:45, given] = scale[:, taken]
            bias_out_ref[0, :, given] = bias[:1, taken]
    for block in range(45):
        words = codes_ref[32 * block : 32 * block + 32, :]
        for place, field_index in enumerate((0, 2, 1, 3)):
            lanes = slice(256 * place, 256 * place + 256)
            scale = scale_ref[block : block + 1, lanes]
            negative, size = twice_fp4(words, field_index)
            scale = jnp.broadcast_to(scale.astype(BF16), size.shape)
            out_ref[0, 32 * block : 32 * block + 32, lanes] = size * jnp.where(
                negative, -scale, scale
            )


def decode_up(codes, exponents, bias):
    rows = codes.shape[0]
    return pl.pallas_call(
        decode_up_kernel,
        grid=(CHUNKS,),
        in_specs=[
            pl.BlockSpec((1440, 256), lambda b: (0, b)),
            pl.BlockSpec((45, 1, 1024), lambda b: (0, 0, b)),
            pl.BlockSpec((1, 1024), lambda b: (0, b)),
        ],
        out_specs=[
            pl.BlockSpec((1, 1440, 1024), lambda b: (b, 0, 0)),
            pl.BlockSpec((1, 1, 1024), lambda b: (b, 0, 0)),
        ],
        out_shape=[
            jax.ShapeDtypeStruct((CHUNKS, rows, 1024), BF16),
            jax.ShapeDtypeStruct((CHUNKS, 1, 1024), F32),
        ],
        scratch_shapes=[pltpu.VMEM((48, 1024), F32)],
        compiler_params=pltpu.CompilerParams(vmem_limit_bytes=LARGE_LIMIT),
        cost_estimate=pl.CostEstimate(flops=60_000_000, bytes_accessed=30_000_000, transcendentals=0),
        name="decode_up",
    )(codes, exponents, bias)


def decode_down_kernel(
    left_ref, middle_ref, right_ref, left_exp_ref, middle_exp_ref, right_exp_ref, out_ref
):
    row = lax.broadcasted_iota(jnp.int32, (16, 512), 0) + 16 * pl.program_id(0)
    column = lax.broadcasted_iota(jnp.int32, (16, 512), 1)
    scales = [
        power_of_two(exponent_ref[:, 0, :], 117, (row < 45) & (column < 1440 - 512 * part))
        for part, exponent_ref in enumerate((left_exp_ref, middle_exp_ref, right_exp_ref))
    ]
    source = lax.broadcasted_iota(jnp.int32, (512, 512), 0)
    target = lax.broadcasted_iota(jnp.int32, (512, 512), 1)
    wanted = 4 * jnp.bitwise_and(source, 127) + jnp.right_shift(source, 7)
    spread = jnp.where(target == wanted, 1.0, 0.0).astype(BF16)
    for parity in range(2):
        for part, codes_ref in enumerate((left_ref, middle_ref, right_ref)):
            piece = codes_ref[pl.ds(parity, 256, 2), :]
            fields = []
            for field_index in range(4):
                negative, size = twice_fp4(piece, field_index)
                fields.append(jnp.where(negative, -size, size))
            natural = jnp.dot(
                jnp.concatenate(fields, axis=1), spread, preferred_element_type=F32
            )
            for block in range(16):
                scale = scales[part][block : block + 1, :]
                row = 256 * parity + 16 * block
                out_ref[pl.program_id(0), row : row + 16, 512 * part : 512 * part + 512] = (
                    natural[16 * block : 16 * block + 16] * scale
                ).astype(BF16)


def decode_down(codes, exponents):
    return pl.pallas_call(
        decode_down_kernel,
        grid=(CHUNKS,),
        in_specs=[
            pl.BlockSpec((512, 128), lambda b: (b, 0)),
            pl.BlockSpec((512, 128), lambda b: (b, 1)),
            pl.BlockSpec((512, 128), lambda b: (b, 2)),
            pl.BlockSpec((16, 1, 512), lambda b: (b, 0, 0)),
            pl.BlockSpec((16, 1, 512), lambda b: (b, 0, 1)),
            pl.BlockSpec((16, 1, 512), lambda b: (b, 0, 2)),
        ],
        out_specs=pl.BlockSpec(memory_space=pltpu.VMEM),
        out_shape=jax.ShapeDtypeStruct((CHUNKS, 512, WIDE), BF16),
        compiler_params=pltpu.CompilerParams(vmem_limit_bytes=SMALL_LIMIT),
        cost_estimate=pl.CostEstimate(flops=60_000_000, bytes_accessed=20_000_000, transcendentals=0),
        name="decode_down",
    )(codes, codes, codes, exponents, exponents, exponents)


def pack_kernel(tokens_ref, ids_ref, level_ref, out_ref):
    for place in range(11):
        block = tokens_ref[128 * place : 128 * place + 128, :].astype(F32)
        out_ref[:, 128 * place : 128 * place + 128] = block.T.astype(BF16)
    expert = lax.broadcasted_iota(jnp.int32, (16, 128), 0)
    named = jnp.zeros((16, 128), F32)
    chosen = jnp.zeros((16, 128), F32)
    whole = jnp.zeros((1, 128), F32)
    for choice in range(4):
        raised = jnp.exp(level_ref[choice : choice + 1, :].astype(F32) / 4.0)
        same = ids_ref[choice : choice + 1, :] == expert
        named = jnp.where(same, 1.0, named)
        chosen = jnp.where(same, raised, chosen)
        whole = whole + raised
    row = lax.broadcasted_iota(jnp.int32, (128, 128), 0)
    column = lax.broadcasted_iota(jnp.int32, (128, 128), 1)
    before = jnp.where(row < column, 1.0, 0.0).astype(BF16)
    rank = jnp.dot(named.astype(BF16), before, preferred_element_type=F32)
    weight = chosen / whole * RETURN_SCALE
    high = weight.astype(BF16).astype(F32)
    last = jnp.concatenate(
        [
            tokens_ref[1408:, :].astype(F32),
            jnp.where(named > 0.0, rank, 128.0),
            high,
            weight - high,
            jnp.zeros((48, 128), F32),
        ],
        axis=0,
    )
    out_ref[:, 1408:] = last.T.astype(BF16)


def pack(tokens, route_ids, route_level):
    return pl.pallas_call(
        pack_kernel,
        grid=(1,),
        in_specs=[
            pl.BlockSpec((1440, 128), lambda i: (0, 0)),
            pl.BlockSpec((4, 128), lambda i: (0, 0)),
            pl.BlockSpec((4, 128), lambda i: (0, 0)),
        ],
        out_specs=pl.BlockSpec(memory_space=pltpu.VMEM),
        out_shape=jax.ShapeDtypeStruct((128, WIDE), BF16),
        compiler_params=pltpu.CompilerParams(vmem_limit_bytes=LARGE_LIMIT),
        name="pack",
    )(tokens.T, route_ids.T, route_level.T)


def relay(block, after):
    return lax.optimization_barrier((block, after))[0]


def combine_weights(shard_ref, place_ref):
    lane = lax.broadcasted_iota(jnp.int32, (128, 384), 1)
    source = lax.broadcasted_iota(jnp.int32, (128, 384), 0)
    expert = jnp.where(jnp.bitwise_and(lane, 127) < MOST, place_ref[0], place_ref[1])
    wanted = 32 + 16 * jnp.right_shift(lane, 7) + expert
    spread = jnp.where(source == wanted, 1.0, 0.0).astype(BF16)
    slot = jnp.bitwise_and(lane[:, :128], MOST - 1).astype(F32)
    meta = jnp.dot(shard_ref[:, 1408:1536], spread, preferred_element_type=F32)
    keep = meta[:, :128] == slot
    parts = [jnp.where(keep, meta[:, 128 * i : 128 * i + 128], 0.0) for i in (1, 2)]
    return jnp.concatenate(parts, axis=1).astype(BF16)


def expert_kernel(count, place_ref, *refs):
    shards = refs[:count]
    (
        first_ref,
        second_ref,
        first_bias_ref,
        second_bias_ref,
        mine_ref,
        other_ref,
        weight_ref,
        rows_ref,
        total_ref,
    ) = refs[count:]
    chunk = pl.program_id(0)
    half = count // 2 * MOST

    @pl.when(chunk == 0)
    def _():
        lane = lax.broadcasted_iota(jnp.int32, (128, 128), 1)
        source = lax.broadcasted_iota(jnp.int32, (128, 128), 0)
        spread = jnp.where(source == 32 + place_ref[0], 1.0, 0.0).astype(BF16)
        slot = jnp.bitwise_and(lane, MOST - 1).astype(F32)
        lower = lane < MOST
        for j in range(0, count, 2):
            picks = []
            for i in range(2):
                at = jnp.dot(shards[j + i][:, 1408:1536], spread, preferred_element_type=F32)
                keep = (at == slot) & (lower if i == 0 else jnp.logical_not(lower))
                picks.append(jnp.where(keep, 1.0, 0.0).astype(BF16))
                if j + i < count // 2:
                    weight_ref[j + i] = combine_weights(shards[j + i], place_ref)
            rows = lax.dot_general(
                jnp.concatenate(picks, axis=0),
                jnp.concatenate([shards[j][...], shards[j + 1][...]], axis=0),
                (((0,), (0,)), ((), ())),
                preferred_element_type=F32,
            )
            rows_ref[MOST * j : MOST * j + 2 * MOST, :] = rows.astype(BF16)

    rows = rows_ref[:, :1440]
    activated = []
    for part in range(2):
        pre = []
        for start in (256 * part, 512 + 256 * part):
            lanes = slice(start, start + 256)
            pre.append(
                jnp.dot(rows, first_ref[chunk, :, lanes], preferred_element_type=F32)
                + first_bias_ref[chunk, :, lanes]
            )
        gate = jnp.minimum(pre[0], 7.0)
        up = jnp.clip(pre[1], -7.0, 7.0)
        activated.append(
            ((up + 1.0) * gate * (0.5 + 0.5 * jnp.tanh(0.851 * gate))).astype(BF16)
        )
    product = jnp.dot(
        jnp.concatenate(activated, axis=1), second_ref[chunk], preferred_element_type=F32
    )

    @pl.when(chunk == 0)
    def _():
        total_ref[...] = product + second_bias_ref[...]

    @pl.when(chunk == 1)
    def _():
        total_ref[...] += product

    @pl.when(chunk == CHUNKS - 1)
    def _():
        done = (total_ref[...] + product).astype(BF16)
        mine_ref[...] = done[:half]
        other_ref[...] = done[half:]


def run_experts(shards, experts, first, second, first_bias, second_bias):
    count = len(shards)
    rows = count * MOST
    half = jax.ShapeDtypeStruct((rows // 2, WIDE), BF16)
    half_spec = pl.BlockSpec(memory_space=pltpu.VMEM)
    return pl.pallas_call(
        functools.partial(expert_kernel, count),
        grid_spec=pltpu.PrefetchScalarGridSpec(
            num_scalar_prefetch=1,
            grid=(CHUNKS,),
            in_specs=[pl.BlockSpec(memory_space=pltpu.VMEM)] * count
            + [
                pl.BlockSpec(memory_space=pltpu.VMEM),
                pl.BlockSpec(memory_space=pltpu.VMEM),
                pl.BlockSpec((CHUNKS, 1, 1024), lambda b, place: (0, 0, 0)),
                pl.BlockSpec((1, WIDE), lambda b, place: (0, 0)),
            ],
            out_specs=[half_spec] * 3,
            scratch_shapes=[pltpu.VMEM((rows, WIDE), BF16), pltpu.VMEM((rows, WIDE), F32)],
        ),
        out_shape=[half, half, jax.ShapeDtypeStruct((count // 2, 128, 256), BF16)],
        compiler_params=pltpu.CompilerParams(vmem_limit_bytes=VMEM_LIMIT),
        cost_estimate=pl.CostEstimate(
            flops=4 * rows * 1440 * 4320, bytes_accessed=30_000_000, transcendentals=0
        ),
        name="experts",
    )(experts, *shards, first, second, first_bias, second_bias)


def combine_kernel(count, weight_ref, mine_ref, other_ref, *outs):
    for j in range(count):
        mine = mine_ref[MOST * j : MOST * j + MOST, :]
        other = other_ref[MOST * j : MOST * j + MOST, :]
        outs[j][...] = jnp.dot(
            weight_ref[j],
            jnp.concatenate([mine, other, mine, other], axis=0),
            preferred_element_type=F32,
        )


def combine(weight, mine, other):
    count = weight.shape[0]
    return pl.pallas_call(
        functools.partial(combine_kernel, count),
        in_specs=[pl.BlockSpec(memory_space=pltpu.VMEM)] * 3,
        out_specs=[pl.BlockSpec(memory_space=pltpu.VMEM)] * count,
        out_shape=[jax.ShapeDtypeStruct((128, WIDE), F32)] * count,
        compiler_params=pltpu.CompilerParams(vmem_limit_bytes=SMALL_LIMIT),
        cost_estimate=pl.CostEstimate(
            flops=2 * count * 128 * 256 * WIDE, bytes_accessed=1_500_000 * count, transcendentals=0
        ),
        name="combine",
    )(weight, mine, other)


def turned(block, cosine, sine_part):
    width = block.shape[1]
    lane = lax.broadcasted_iota(jnp.int32, block.shape, 1)
    first = jnp.bitwise_and(lane, 63) < 32
    swapped = jnp.where(first, pltpu.roll(block, width - 32, 1), pltpu.roll(block, 32, 1))
    copies = width // 128
    cosine = jnp.concatenate([cosine] * copies, axis=1)
    sine_part = jnp.concatenate([sine_part] * copies, axis=1)
    return block * cosine + swapped * sine_part


def mix_kernel(
    tokens_ref, mixture_ref, gain_ref, key_ref, value_ref, cos_ref, sin_ref, out_ref, normed_ref, kv_ref
):
    rounded = (tokens_ref[...].astype(F32) + mixture_ref[...]).astype(BF16).astype(F32)
    for place in range(11):
        rows = slice(128 * place, 128 * place + 128)
        out_ref[rows, :] = rounded[:, rows].T.astype(BF16)
    out_ref[1408:, :] = rounded[:, 1408:].T[:32].astype(BF16)
    widened = rounded[:, :1440]
    squares = jnp.sum(widened * widened, axis=1, keepdims=True) / 1440.0
    normed = (widened * lax.rsqrt(squares + 1e-05) * gain_ref[...].astype(F32)).astype(BF16)
    normed_ref[...] = normed
    keys = jnp.dot(normed, key_ref[...], preferred_element_type=F32)
    kv_ref[:, :256] = turned(keys, cos_ref[...], sin_ref[...]).astype(BF16)
    kv_ref[:, 256:] = jnp.dot(normed, value_ref[...], preferred_element_type=F32).astype(BF16)


def mix(tokens, mixture, gain, key_matrix, value_matrix, cosine, sine_part):
    return pl.pallas_call(
        mix_kernel,
        out_shape=[
            jax.ShapeDtypeStruct((1440, 128), BF16),
            jax.ShapeDtypeStruct((128, 1440), BF16),
            jax.ShapeDtypeStruct((128, 512), BF16),
        ],
        compiler_params=pltpu.CompilerParams(vmem_limit_bytes=SMALL_LIMIT),
        cost_estimate=pl.CostEstimate(
            flops=2 * 128 * 1440 * 512, bytes_accessed=3_000_000, transcendentals=0
        ),
        name="mix",
    )(tokens, mixture, gain, key_matrix, value_matrix, cosine, sine_part)


def queries_kernel(normed_ref, weight_ref, cos_ref, sin_ref, out_ref):
    projected = jnp.dot(normed_ref[...], weight_ref[...], preferred_element_type=F32)
    rotated = turned(projected, cos_ref[...], sin_ref[...])
    scaled = (rotated.astype(BF16).astype(F32) * 0.125).astype(BF16)
    for pair in range(4):
        out_ref[0, 128 * pair : 128 * pair + 128, :] = scaled[:, 128 * pair : 128 * pair + 128]


def queries(normed, weight, cosine, sine_part):
    return pl.pallas_call(
        queries_kernel,
        grid=(4,),
        in_specs=[
            pl.BlockSpec((128, 1440), lambda g: (0, 0)),
            pl.BlockSpec((1440, 512), lambda g: (0, g)),
            pl.BlockSpec((128, 128), lambda g: (0, 0)),
            pl.BlockSpec((128, 128), lambda g: (0, 0)),
        ],
        out_specs=pl.BlockSpec((1, 512, 128), lambda g: (g, 0, 0)),
        out_shape=jax.ShapeDtypeStruct((4, 512, 128), BF16),
        compiler_params=pltpu.CompilerParams(vmem_limit_bytes=SMALL_LIMIT),
        cost_estimate=pl.CostEstimate(
            flops=2 * 128 * 1440 * 2048, bytes_accessed=7_000_000, transcendentals=0
        ),
        name="queries",
    )(normed, weight, cosine, sine_part)


def attend_kernel(index_ref, sinks_ref, queries_ref, own_ref, halo_ref, out_ref):
    lane = lax.broadcasted_iota(jnp.int32, (128, 128), 1)
    lower = lane < 64

    def doubled(block, odd):
        block = block.astype(F32)
        if odd:
            high = jnp.where(lower, 0.0, block)
            low = pltpu.roll(high, 64, 1)
        else:
            low = jnp.where(lower, block, 0.0)
            high = pltpu.roll(low, 64, 1)
        return jnp.concatenate([low, high], axis=0).astype(BF16)

    row = lax.broadcasted_iota(jnp.int32, (128, 256), 0)
    column = jnp.bitwise_and(lax.broadcasted_iota(jnp.int32, (128, 256), 1), 127)
    mine = column <= row
    allowed = mine | jnp.broadcast_to(index_ref[0] > 0, mine.shape)
    for group in range(4):
        start = 128 * (group // 2)
        odd = group % 2 == 1
        query = queries_ref[group]
        across = (((1,), (1,)), ((), ()))
        here = lax.dot_general(
            query, doubled(own_ref[:, start : start + 128], odd), across, preferred_element_type=F32
        )
        there = lax.dot_general(
            query, doubled(halo_ref[:, start : start + 128], odd), across, preferred_element_type=F32
        )
        here_probs = []
        there_probs = []
        for pair in range(4):
            rows = slice(128 * pair, 128 * pair + 128)
            scores = jnp.where(mine, here[rows], there[rows])
            scores = jnp.where(allowed, scores, -1e30)
            halves = []
            for side in range(2):
                part = scores[:, 128 * side : 128 * side + 128]
                sink = sinks_ref[8 * group + 2 * pair + side]
                top = jnp.maximum(jnp.max(part, axis=1, keepdims=True), sink)
                weights = jnp.exp(part - top)
                whole = jnp.exp(sink - top) + jnp.sum(weights, axis=1, keepdims=True)
                halves.append(weights * (1.0 / whole))
            probs = jnp.concatenate(halves, axis=1)
            here_probs.append(jnp.where(mine, probs, 0.0).astype(BF16))
            there_probs.append(jnp.where(mine, 0.0, probs).astype(BF16))
        mixed = jnp.dot(
            jnp.concatenate(here_probs, axis=0),
            doubled(own_ref[:, 256 + start : 384 + start], odd),
            preferred_element_type=F32,
        ) + jnp.dot(
            jnp.concatenate(there_probs, axis=0),
            doubled(halo_ref[:, 256 + start : 384 + start], odd),
            preferred_element_type=F32,
        )
        for pair in range(4):
            place = 512 * group + 128 * pair
            out_ref[:, place : place + 128] = mixed[128 * pair : 128 * pair + 128].astype(BF16)


def attend(index, sinks, query, own, halo):
    return pl.pallas_call(
        attend_kernel,
        in_specs=[
            pl.BlockSpec(memory_space=pltpu.SMEM),
            pl.BlockSpec(memory_space=pltpu.SMEM),
            pl.BlockSpec(memory_space=pltpu.VMEM),
            pl.BlockSpec(memory_space=pltpu.VMEM),
            pl.BlockSpec(memory_space=pltpu.VMEM),
        ],
        out_specs=pl.BlockSpec(memory_space=pltpu.VMEM),
        out_shape=jax.ShapeDtypeStruct((128, 2048), BF16),
        compiler_params=pltpu.CompilerParams(vmem_limit_bytes=SMALL_LIMIT),
        cost_estimate=pl.CostEstimate(
            flops=2 * 32 * 128 * 256 * 128, bytes_accessed=1_500_000, transcendentals=1_000_000
        ),
        name="attend",
    )(index, sinks, query, own, halo)


def body(
    tokens,
    route_ids,
    route_level,
    gate_up_codes,
    gate_up_scale,
    gate_up_bias,
    down_codes,
    down_scale,
    down_bias,
    attn_gain,
    query_weight,
    key_matrix,
    value_matrix,
    sinks,
):
    own_tokens, width = tokens.shape
    group_size = lax.axis_size("expert")
    far = group_size // 4
    device_index = lax.axis_index("expert")
    core = device_index % 2

    partner = [(i, i ^ 1) for i in range(group_size)]

    def swap(block):
        return lax.ppermute(block, "expert", partner)

    def inward(block, across):
        route = []
        for i in range(group_size):
            goal = (i + (-2 if i % 2 else 2)) % group_size
            route.append((i ^ 1 if across else i, goal))
        return lax.ppermute(block, "expert", route)

    packed = pack(tokens, route_ids, route_level)

    second = decode_down(down_codes[0], down_scale.transpose(1, 0, 2))
    first, first_bias = decode_up(
        gate_up_codes[0], gate_up_scale.transpose(1, 0, 2), gate_up_bias
    )
    second_bias = jnp.pad(down_bias.astype(F32), ((0, 0), (0, WIDE - width)))
    experts = jnp.stack([device_index, device_index + 1 - 2 * core]).astype(jnp.int32)

    def serve(blocks, after):
        return run_experts(
            blocks + [swap(block) for block in blocks],
            relay(experts, after),
            first,
            second,
            first_bias,
            second_bias,
        )

    def gather(served):
        rows, given, weight = served
        return combine(weight, rows, swap(given))

    same = [packed, inward(packed, False)]
    cross = [packed, inward(packed, True)]
    same[1] = relay(same[1], first)
    same.append(inward(same[1], False))
    cross.append(inward(cross[1], False))
    same[2] = relay(same[2], second)
    same.append(inward(same[2], False))
    cross.append(inward(cross[2], False))
    served_near = serve([same[1], cross[1], packed], packed)
    same[3] = relay(same[3], served_near)
    same.append(inward(same[3], False))
    served_middle = serve([same[2], cross[2]], served_near)
    same[far] = relay(same[far], served_middle)
    served_far = serve([same[far], same[far - 1], cross[far - 1]], served_middle)
    same_far, same_third, cross_third = gather(served_far)
    same_near = [None, None, None]
    cross_near = [None, None, None]
    same_near[2], cross_near[2] = gather(relay(served_middle, same_far))
    same_near[1], cross_near[1], own = gather(relay(served_near, same_far))

    half_dim = HEAD_SIZE // 2
    frequency = jnp.power(
        jnp.float32(150000.0), -2.0 * jnp.arange(half_dim, dtype=F32) / (2 * half_dim)
    )
    token_positions = device_index * own_tokens + jnp.arange(own_tokens, dtype=jnp.int32)
    angles = token_positions.astype(F32)[:, None] * frequency[None, :]
    cosine = jnp.tile(jnp.cos(angles), (1, 4))
    sine_part = jnp.sin(angles)
    sine_part = jnp.concatenate([-sine_part, sine_part, -sine_part, sine_part], axis=1)

    def onward(block, across):
        route = []
        for i in range(group_size):
            goal = (i + (2 if i % 2 else -2)) % group_size
            route.append((i, goal ^ 1 if across else goal))
        return lax.ppermute(block.astype(jnp.float16), "expert", route).astype(F32)

    from_same = onward(same_far, False)
    from_cross = onward(cross_third, False)
    from_same = onward(same_third + from_same, False)
    from_same = onward(same_near[2] + from_same, False)
    from_cross = onward(cross_near[2] + from_cross, False)
    from_same = onward(same_near[1] + from_same, False)
    from_cross = onward(cross_near[1] + from_cross, True)
    mixture = (own + from_same + from_cross) * (1.0 / RETURN_SCALE)

    block_out, normed, own_kv = mix(
        packed, mixture, attn_gain[None], key_matrix, value_matrix, cosine, sine_part
    )
    ahead = [(i, i + 1) for i in range(group_size - 1)]
    halo_kv = lax.ppermute(own_kv, "expert", ahead)
    query = queries(normed, query_weight, cosine, sine_part)
    attended = attend(device_index.reshape(1), sinks, query, own_kv, halo_kv)
    return (block_out.T, attended)


def solution(mesh):
    in_specs = (
        P(("dp", "expert"), None),
        P(("dp", "expert"), None),
        P(("dp", "expert"), None),
        P("expert", None, None),
        P("expert", None, None),
        P("expert", None),
        P("expert", None, None),
        P("expert", None, None),
        P("expert", None),
        P(),
        P(),
        P(),
        P(),
        P(),
    )
    out_specs = (P(("dp", "expert"), None), P(("dp", "expert"), None))
    return jax.shard_map(body, mesh=mesh, in_specs=in_specs, out_specs=out_specs, check_vma=False)
```

```python
import functools

import jax
import jax.numpy as jnp
from jax import lax
from jax.experimental import pallas as pl
from jax.experimental.pallas import tpu as pltpu
from jax.sharding import PartitionSpec as P

HEAD_SIZE = 64
WINDOW_LENGTH = 128
MOST = 64
WIDE = 1536
CHUNKS = 3
RETURN_SCALE = 8.0
LARGE_LIMIT = 56 * 1024 * 1024
VMEM_LIMIT = 22 * 1024 * 1024
SMALL_LIMIT = 16 * 1024 * 1024
F32 = jnp.float32
BF16 = jnp.bfloat16


def twice_fp4(words, field_index):
    field = jnp.bitwise_and(jnp.right_shift(words, 4 * field_index), 15).astype(F32).astype(BF16)
    negative = field >= 8
    low = jnp.where(negative, field - 8, field)
    return negative, jnp.maximum(jnp.maximum(low, 2 * low - 4), 4 * low - 16)


def power_of_two(exponents, least, valid):
    step = exponents - least
    scale = jnp.where(step == 0, 1.0, jnp.where(step == 1, 2.0, jnp.where(step == 2, 4.0, 8.0)))
    return jnp.where(valid, scale * 2.0 ** (least - 128), 0.0)


def decode_up_kernel(codes_ref, exponent_ref, bias_ref, out_ref, bias_out_ref, scale_ref):
    chunk = pl.program_id(0)
    source = lax.broadcasted_iota(jnp.int32, (512, 512), 0)
    target = lax.broadcasted_iota(jnp.int32, (512, 512), 1)
    wanted = 128 * jnp.bitwise_and(source, 3) + jnp.right_shift(source, 2)
    spread = jnp.where(target == wanted, 1.0, 0.0).astype(BF16)
    for half in range(2):
        lanes = slice(512 * half, 512 * half + 512)
        left = 2880 - 1024 * chunk - 512 * half
        column = lax.broadcasted_iota(jnp.int32, (45, 512), 1)
        scale = power_of_two(exponent_ref[:, lanes], 119, column < left)
        scale = jnp.dot(scale.astype(BF16), spread, preferred_element_type=F32)
        bias = jnp.where(column[:1] < left, bias_ref[:, lanes].astype(F32), 0.0)
        bias = jnp.broadcast_to(bias, (16, 512)).astype(BF16)
        bias = jnp.dot(bias, spread, preferred_element_type=F32)
        for place, field_index in enumerate((0, 2, 1, 3)):
            taken = slice(128 * field_index, 128 * field_index + 128)
            given = slice(256 * place + 128 * half, 256 * place + 128 * half + 128)
            scale_ref[:45, given] = scale[:, taken]
            bias_out_ref[0, :, given] = bias[:1, taken]
    for block in range(45):
        words = codes_ref[32 * block : 32 * block + 32, :]
        for place, field_index in enumerate((0, 2, 1, 3)):
            lanes = slice(256 * place, 256 * place + 256)
            scale = scale_ref[block : block + 1, lanes]
            negative, size = twice_fp4(words, field_index)
            scale = jnp.broadcast_to(scale.astype(BF16), size.shape)
            out_ref[0, 32 * block : 32 * block + 32, lanes] = size * jnp.where(
                negative, -scale, scale
            )


def decode_up(codes, exponents, bias):
    rows = codes.shape[0]
    return pl.pallas_call(
        decode_up_kernel,
        grid=(CHUNKS,),
        in_specs=[
            pl.BlockSpec((1440, 256), lambda b: (0, b)),
            pl.BlockSpec((45, 1024), lambda b: (0, b)),
            pl.BlockSpec((1, 1024), lambda b: (0, b)),
        ],
        out_specs=[
            pl.BlockSpec((1, 1440, 1024), lambda b: (b, 0, 0)),
            pl.BlockSpec((1, 1, 1024), lambda b: (b, 0, 0)),
        ],
        out_shape=[
            jax.ShapeDtypeStruct((CHUNKS, rows, 1024), BF16),
            jax.ShapeDtypeStruct((CHUNKS, 1, 1024), F32),
        ],
        scratch_shapes=[pltpu.VMEM((48, 1024), F32)],
        compiler_params=pltpu.CompilerParams(vmem_limit_bytes=LARGE_LIMIT),
        cost_estimate=pl.CostEstimate(flops=60_000_000, bytes_accessed=30_000_000, transcendentals=0),
        name="decode_up",
    )(codes, exponents, bias)


def decode_down_kernel(
    left_ref, middle_ref, right_ref, left_exp_ref, middle_exp_ref, right_exp_ref, out_ref
):
    row = lax.broadcasted_iota(jnp.int32, (16, 512), 0) + 16 * pl.program_id(0)
    column = lax.broadcasted_iota(jnp.int32, (16, 512), 1)
    scales = [
        power_of_two(exponent_ref[...], 117, (row < 45) & (column < 1440 - 512 * part))
        for part, exponent_ref in enumerate((left_exp_ref, middle_exp_ref, right_exp_ref))
    ]
    source = lax.broadcasted_iota(jnp.int32, (512, 512), 0)
    target = lax.broadcasted_iota(jnp.int32, (512, 512), 1)
    wanted = 4 * jnp.bitwise_and(source, 127) + jnp.right_shift(source, 7)
    spread = jnp.where(target == wanted, 1.0, 0.0).astype(BF16)
    for parity in range(2):
        for part, codes_ref in enumerate((left_ref, middle_ref, right_ref)):
            piece = codes_ref[pl.ds(parity, 256, 2), :]
            fields = []
            for field_index in range(4):
                negative, size = twice_fp4(piece, field_index)
                fields.append(jnp.where(negative, -size, size))
            natural = jnp.dot(
                jnp.concatenate(fields, axis=1), spread, preferred_element_type=F32
            )
            for block in range(16):
                scale = scales[part][block : block + 1, :]
                row = 256 * parity + 16 * block
                out_ref[pl.program_id(0), row : row + 16, 512 * part : 512 * part + 512] = (
                    natural[16 * block : 16 * block + 16] * scale
                ).astype(BF16)


def decode_down(codes, exponents):
    return pl.pallas_call(
        decode_down_kernel,
        grid=(CHUNKS,),
        in_specs=[
            pl.BlockSpec((512, 128), lambda b: (b, 0)),
            pl.BlockSpec((512, 128), lambda b: (b, 1)),
            pl.BlockSpec((512, 128), lambda b: (b, 2)),
            pl.BlockSpec((16, 512), lambda b: (b, 0)),
            pl.BlockSpec((16, 512), lambda b: (b, 1)),
            pl.BlockSpec((16, 512), lambda b: (b, 2)),
        ],
        out_specs=pl.BlockSpec(memory_space=pltpu.VMEM),
        out_shape=jax.ShapeDtypeStruct((CHUNKS, 512, WIDE), BF16),
        compiler_params=pltpu.CompilerParams(vmem_limit_bytes=SMALL_LIMIT),
        cost_estimate=pl.CostEstimate(flops=60_000_000, bytes_accessed=20_000_000, transcendentals=0),
        name="decode_down",
    )(codes, codes, codes, exponents, exponents, exponents)


def pack_kernel(tokens_ref, ids_ref, level_ref, out_ref):
    for place in range(11):
        block = tokens_ref[128 * place : 128 * place + 128, :].astype(F32)
        out_ref[:, 128 * place : 128 * place + 128] = block.T.astype(BF16)
    expert = lax.broadcasted_iota(jnp.int32, (16, 128), 0)
    named = jnp.zeros((16, 128), F32)
    chosen = jnp.zeros((16, 128), F32)
    whole = jnp.zeros((1, 128), F32)
    for choice in range(4):
        raised = jnp.exp(level_ref[choice : choice + 1, :].astype(F32) / 4.0)
        same = ids_ref[choice : choice + 1, :] == expert
        named = jnp.where(same, 1.0, named)
        chosen = jnp.where(same, raised, chosen)
        whole = whole + raised
    row = lax.broadcasted_iota(jnp.int32, (128, 128), 0)
    column = lax.broadcasted_iota(jnp.int32, (128, 128), 1)
    before = jnp.where(row < column, 1.0, 0.0).astype(BF16)
    rank = jnp.dot(named.astype(BF16), before, preferred_element_type=F32)
    weight = chosen / whole * RETURN_SCALE
    high = weight.astype(BF16).astype(F32)
    last = jnp.concatenate(
        [
            tokens_ref[1408:, :].astype(F32),
            jnp.where(named > 0.0, rank, 128.0),
            high,
            weight - high,
            jnp.zeros((48, 128), F32),
        ],
        axis=0,
    )
    out_ref[:, 1408:] = last.T.astype(BF16)


def pack(tokens, route_ids, route_level):
    return pl.pallas_call(
        pack_kernel,
        grid=(1,),
        in_specs=[
            pl.BlockSpec((1440, 128), lambda i: (0, 0)),
            pl.BlockSpec((4, 128), lambda i: (0, 0)),
            pl.BlockSpec((4, 128), lambda i: (0, 0)),
        ],
        out_specs=pl.BlockSpec(memory_space=pltpu.VMEM),
        out_shape=jax.ShapeDtypeStruct((128, WIDE), BF16),
        compiler_params=pltpu.CompilerParams(vmem_limit_bytes=LARGE_LIMIT),
        name="pack",
    )(tokens.T, route_ids.T, route_level.T)


def relay(block, after):
    return lax.optimization_barrier((block, after))[0]


def combine_weights(shard_ref, place_ref):
    lane = lax.broadcasted_iota(jnp.int32, (128, 384), 1)
    source = lax.broadcasted_iota(jnp.int32, (128, 384), 0)
    expert = jnp.where(jnp.bitwise_and(lane, 127) < MOST, place_ref[0], place_ref[1])
    wanted = 32 + 16 * jnp.right_shift(lane, 7) + expert
    spread = jnp.where(source == wanted, 1.0, 0.0).astype(BF16)
    slot = jnp.bitwise_and(lane[:, :128], MOST - 1).astype(F32)
    meta = jnp.dot(shard_ref[:, 1408:1536], spread, preferred_element_type=F32)
    keep = meta[:, :128] == slot
    parts = [jnp.where(keep, meta[:, 128 * i : 128 * i + 128], 0.0) for i in (1, 2)]
    return jnp.concatenate(parts, axis=1).astype(BF16)


def expert_kernel(count, place_ref, *refs):
    shards = refs[:count]
    (
        first_ref,
        second_ref,
        first_bias_ref,
        second_bias_ref,
        mine_ref,
        other_ref,
        weight_ref,
        rows_ref,
        total_ref,
    ) = refs[count:]
    chunk = pl.program_id(0)
    half = count // 2 * MOST

    @pl.when(chunk == 0)
    def _():
        lane = lax.broadcasted_iota(jnp.int32, (128, 128), 1)
        source = lax.broadcasted_iota(jnp.int32, (128, 128), 0)
        spread = jnp.where(source == 32 + place_ref[0], 1.0, 0.0).astype(BF16)
        slot = jnp.bitwise_and(lane, MOST - 1).astype(F32)
        lower = lane < MOST
        for j in range(0, count, 2):
            picks = []
            for i in range(2):
                at = jnp.dot(shards[j + i][:, 1408:1536], spread, preferred_element_type=F32)
                keep = (at == slot) & (lower if i == 0 else jnp.logical_not(lower))
                picks.append(jnp.where(keep, 1.0, 0.0).astype(BF16))
                if j + i < count // 2:
                    weight_ref[j + i] = combine_weights(shards[j + i], place_ref)
            rows = lax.dot_general(
                jnp.concatenate(picks, axis=0),
                jnp.concatenate([shards[j][...], shards[j + 1][...]], axis=0),
                (((0,), (0,)), ((), ())),
                preferred_element_type=F32,
            )
            rows_ref[MOST * j : MOST * j + 2 * MOST, :] = rows.astype(BF16)

    rows = rows_ref[:, :1440]
    activated = []
    for part in range(2):
        pre = []
        for start in (256 * part, 512 + 256 * part):
            lanes = slice(start, start + 256)
            pre.append(
                jnp.dot(rows, first_ref[chunk, :, lanes], preferred_element_type=F32)
                + first_bias_ref[chunk, :, lanes]
            )
        gate = jnp.minimum(pre[0], 7.0)
        up = jnp.clip(pre[1], -7.0, 7.0)
        activated.append(
            ((up + 1.0) * gate * (0.5 + 0.5 * jnp.tanh(0.851 * gate))).astype(BF16)
        )
    product = jnp.dot(
        jnp.concatenate(activated, axis=1), second_ref[chunk], preferred_element_type=F32
    )

    @pl.when(chunk == 0)
    def _():
        total_ref[...] = product + second_bias_ref[...]

    @pl.when(chunk == 1)
    def _():
        total_ref[...] += product

    @pl.when(chunk == CHUNKS - 1)
    def _():
        done = (total_ref[...] + product).astype(BF16)
        mine_ref[...] = done[:half]
        other_ref[...] = done[half:]


def run_experts(shards, experts, first, second, first_bias, second_bias):
    count = len(shards)
    rows = count * MOST
    half = jax.ShapeDtypeStruct((rows // 2, WIDE), BF16)
    half_spec = pl.BlockSpec(memory_space=pltpu.VMEM)
    return pl.pallas_call(
        functools.partial(expert_kernel, count),
        grid_spec=pltpu.PrefetchScalarGridSpec(
            num_scalar_prefetch=1,
            grid=(CHUNKS,),
            in_specs=[pl.BlockSpec(memory_space=pltpu.VMEM)] * count
            + [
                pl.BlockSpec(memory_space=pltpu.VMEM),
                pl.BlockSpec(memory_space=pltpu.VMEM),
                pl.BlockSpec((CHUNKS, 1, 1024), lambda b, place: (0, 0, 0)),
                pl.BlockSpec((1, WIDE), lambda b, place: (0, 0)),
            ],
            out_specs=[half_spec] * 3,
            scratch_shapes=[pltpu.VMEM((rows, WIDE), BF16), pltpu.VMEM((rows, WIDE), F32)],
        ),
        out_shape=[half, half, jax.ShapeDtypeStruct((count // 2, 128, 256), BF16)],
        compiler_params=pltpu.CompilerParams(vmem_limit_bytes=VMEM_LIMIT),
        cost_estimate=pl.CostEstimate(
            flops=4 * rows * 1440 * 4320, bytes_accessed=30_000_000, transcendentals=0
        ),
        name="experts",
    )(experts, *shards, first, second, first_bias, second_bias)


def combine_kernel(count, weight_ref, mine_ref, other_ref, *outs):
    for j in range(count):
        mine = mine_ref[MOST * j : MOST * j + MOST, :]
        other = other_ref[MOST * j : MOST * j + MOST, :]
        outs[j][...] = jnp.dot(
            weight_ref[j],
            jnp.concatenate([mine, other, mine, other], axis=0),
            preferred_element_type=F32,
        )


def combine(weight, mine, other):
    count = weight.shape[0]
    return pl.pallas_call(
        functools.partial(combine_kernel, count),
        in_specs=[pl.BlockSpec(memory_space=pltpu.VMEM)] * 3,
        out_specs=[pl.BlockSpec(memory_space=pltpu.VMEM)] * count,
        out_shape=[jax.ShapeDtypeStruct((128, WIDE), F32)] * count,
        compiler_params=pltpu.CompilerParams(vmem_limit_bytes=SMALL_LIMIT),
        cost_estimate=pl.CostEstimate(
            flops=2 * count * 128 * 256 * WIDE, bytes_accessed=1_500_000 * count, transcendentals=0
        ),
        name="combine",
    )(weight, mine, other)


def turned(block, cosine, sine_part):
    width = block.shape[1]
    lane = lax.broadcasted_iota(jnp.int32, block.shape, 1)
    first = jnp.bitwise_and(lane, 63) < 32
    swapped = jnp.where(first, pltpu.roll(block, width - 32, 1), pltpu.roll(block, 32, 1))
    copies = width // 128
    cosine = jnp.concatenate([cosine] * copies, axis=1)
    sine_part = jnp.concatenate([sine_part] * copies, axis=1)
    return block * cosine + swapped * sine_part


def mix_kernel(
    tokens_ref, mixture_ref, gain_ref, key_ref, value_ref, cos_ref, sin_ref, out_ref, normed_ref, kv_ref
):
    rounded = (tokens_ref[...].astype(F32) + mixture_ref[...]).astype(BF16).astype(F32)
    for place in range(11):
        rows = slice(128 * place, 128 * place + 128)
        out_ref[rows, :] = rounded[:, rows].T.astype(BF16)
    out_ref[1408:, :] = rounded[:, 1408:].T[:32].astype(BF16)
    widened = rounded[:, :1440]
    squares = jnp.sum(widened * widened, axis=1, keepdims=True) / 1440.0
    normed = (widened * lax.rsqrt(squares + 1e-05) * gain_ref[...].astype(F32)).astype(BF16)
    normed_ref[...] = normed
    keys = jnp.dot(normed, key_ref[...], preferred_element_type=F32)
    kv_ref[:, :256] = turned(keys, cos_ref[...], sin_ref[...]).astype(BF16)
    kv_ref[:, 256:] = jnp.dot(normed, value_ref[...], preferred_element_type=F32).astype(BF16)


def mix(tokens, mixture, gain, key_matrix, value_matrix, cosine, sine_part):
    return pl.pallas_call(
        mix_kernel,
        out_shape=[
            jax.ShapeDtypeStruct((1440, 128), BF16),
            jax.ShapeDtypeStruct((128, 1440), BF16),
            jax.ShapeDtypeStruct((128, 512), BF16),
        ],
        compiler_params=pltpu.CompilerParams(vmem_limit_bytes=SMALL_LIMIT),
        cost_estimate=pl.CostEstimate(
            flops=2 * 128 * 1440 * 512, bytes_accessed=3_000_000, transcendentals=0
        ),
        name="mix",
    )(tokens, mixture, gain, key_matrix, value_matrix, cosine, sine_part)


def queries_kernel(normed_ref, weight_ref, cos_ref, sin_ref, out_ref):
    projected = jnp.dot(normed_ref[...], weight_ref[...], preferred_element_type=F32)
    rotated = turned(projected, cos_ref[...], sin_ref[...])
    scaled = (rotated.astype(BF16).astype(F32) * 0.125).astype(BF16)
    for pair in range(4):
        out_ref[0, 128 * pair : 128 * pair + 128, :] = scaled[:, 128 * pair : 128 * pair + 128]


def queries(normed, weight, cosine, sine_part):
    return pl.pallas_call(
        queries_kernel,
        grid=(4,),
        in_specs=[
            pl.BlockSpec((128, 1440), lambda g: (0, 0)),
            pl.BlockSpec((1440, 512), lambda g: (0, g)),
            pl.BlockSpec((128, 128), lambda g: (0, 0)),
            pl.BlockSpec((128, 128), lambda g: (0, 0)),
        ],
        out_specs=pl.BlockSpec((1, 512, 128), lambda g: (g, 0, 0)),
        out_shape=jax.ShapeDtypeStruct((4, 512, 128), BF16),
        compiler_params=pltpu.CompilerParams(vmem_limit_bytes=SMALL_LIMIT),
        cost_estimate=pl.CostEstimate(
            flops=2 * 128 * 1440 * 2048, bytes_accessed=7_000_000, transcendentals=0
        ),
        name="queries",
    )(normed, weight, cosine, sine_part)


def attend_kernel(index_ref, sinks_ref, queries_ref, own_ref, halo_ref, out_ref):
    lane = lax.broadcasted_iota(jnp.int32, (128, 128), 1)
    lower = lane < 64

    def doubled(block, odd):
        block = block.astype(F32)
        if odd:
            high = jnp.where(lower, 0.0, block)
            low = pltpu.roll(high, 64, 1)
        else:
            low = jnp.where(lower, block, 0.0)
            high = pltpu.roll(low, 64, 1)
        return jnp.concatenate([low, high], axis=0).astype(BF16)

    row = lax.broadcasted_iota(jnp.int32, (128, 256), 0)
    column = jnp.bitwise_and(lax.broadcasted_iota(jnp.int32, (128, 256), 1), 127)
    mine = column <= row
    allowed = mine | jnp.broadcast_to(index_ref[0] > 0, mine.shape)
    for group in range(4):
        start = 128 * (group // 2)
        odd = group % 2 == 1
        query = queries_ref[group]
        across = (((1,), (1,)), ((), ()))
        here = lax.dot_general(
            query, doubled(own_ref[:, start : start + 128], odd), across, preferred_element_type=F32
        )
        there = lax.dot_general(
            query, doubled(halo_ref[:, start : start + 128], odd), across, preferred_element_type=F32
        )
        here_probs = []
        there_probs = []
        for pair in range(4):
            rows = slice(128 * pair, 128 * pair + 128)
            scores = jnp.where(mine, here[rows], there[rows])
            scores = jnp.where(allowed, scores, -1e30)
            halves = []
            for side in range(2):
                part = scores[:, 128 * side : 128 * side + 128]
                sink = sinks_ref[8 * group + 2 * pair + side]
                top = jnp.maximum(jnp.max(part, axis=1, keepdims=True), sink)
                weights = jnp.exp(part - top)
                whole = jnp.exp(sink - top) + jnp.sum(weights, axis=1, keepdims=True)
                halves.append(weights * (1.0 / whole))
            probs = jnp.concatenate(halves, axis=1)
            here_probs.append(jnp.where(mine, probs, 0.0).astype(BF16))
            there_probs.append(jnp.where(mine, 0.0, probs).astype(BF16))
        mixed = jnp.dot(
            jnp.concatenate(here_probs, axis=0),
            doubled(own_ref[:, 256 + start : 384 + start], odd),
            preferred_element_type=F32,
        ) + jnp.dot(
            jnp.concatenate(there_probs, axis=0),
            doubled(halo_ref[:, 256 + start : 384 + start], odd),
            preferred_element_type=F32,
        )
        for pair in range(4):
            place = 512 * group + 128 * pair
            out_ref[:, place : place + 128] = mixed[128 * pair : 128 * pair + 128].astype(BF16)


def attend(index, sinks, query, own, halo):
    return pl.pallas_call(
        attend_kernel,
        in_specs=[
            pl.BlockSpec(memory_space=pltpu.SMEM),
            pl.BlockSpec(memory_space=pltpu.SMEM),
            pl.BlockSpec(memory_space=pltpu.VMEM),
            pl.BlockSpec(memory_space=pltpu.VMEM),
            pl.BlockSpec(memory_space=pltpu.VMEM),
        ],
        out_specs=pl.BlockSpec(memory_space=pltpu.VMEM),
        out_shape=jax.ShapeDtypeStruct((128, 2048), BF16),
        compiler_params=pltpu.CompilerParams(vmem_limit_bytes=SMALL_LIMIT),
        cost_estimate=pl.CostEstimate(
            flops=2 * 32 * 128 * 256 * 128, bytes_accessed=1_500_000, transcendentals=1_000_000
        ),
        name="attend",
    )(index, sinks, query, own, halo)


def body(
    tokens,
    route_ids,
    route_level,
    gate_up_codes,
    gate_up_scale,
    gate_up_bias,
    down_codes,
    down_scale,
    down_bias,
    attn_gain,
    query_weight,
    key_matrix,
    value_matrix,
    sinks,
):
    own_tokens, width = tokens.shape
    group_size = lax.axis_size("expert")
    far = group_size // 4
    device_index = lax.axis_index("expert")
    core = device_index % 2

    partner = [(i, i ^ 1) for i in range(group_size)]

    def swap(block):
        return lax.ppermute(block, "expert", partner)

    def inward(block, across):
        route = []
        for i in range(group_size):
            goal = (i + (-2 if i % 2 else 2)) % group_size
            route.append((i ^ 1 if across else i, goal))
        return lax.ppermute(block, "expert", route)

    packed = pack(tokens, route_ids, route_level)

    second = decode_down(down_codes[0], down_scale[0])
    first, first_bias = decode_up(gate_up_codes[0], gate_up_scale[0], gate_up_bias)
    second_bias = jnp.pad(down_bias.astype(F32), ((0, 0), (0, WIDE - width)))
    experts = jnp.stack([device_index, device_index + 1 - 2 * core]).astype(jnp.int32)

    def serve(blocks, after):
        return run_experts(
            blocks + [swap(block) for block in blocks],
            relay(experts, after),
            first,
            second,
            first_bias,
            second_bias,
        )

    def gather(served):
        rows, given, weight = served
        return combine(weight, rows, swap(given))

    same = [packed, inward(packed, False)]
    cross = [packed, inward(packed, True)]
    same[1] = relay(same[1], first)
    same.append(inward(same[1], False))
    cross.append(inward(cross[1], False))
    same[2] = relay(same[2], second)
    same.append(inward(same[2], False))
    cross.append(inward(cross[2], False))
    served_near = serve([same[1], cross[1], packed], packed)
    same[3] = relay(same[3], served_near)
    same.append(inward(same[3], False))
    served_middle = serve([same[2], cross[2]], served_near)
    same[far] = relay(same[far], served_middle)
    served_far = serve([same[far], same[far - 1], cross[far - 1]], served_middle)
    same_far, same_third, cross_third = gather(served_far)
    same_near = [None, None, None]
    cross_near = [None, None, None]
    same_near[2], cross_near[2] = gather(relay(served_middle, same_far))
    same_near[1], cross_near[1], own = gather(relay(served_near, same_far))

    half_dim = HEAD_SIZE // 2
    frequency = jnp.power(
        jnp.float32(150000.0), -2.0 * jnp.arange(half_dim, dtype=F32) / (2 * half_dim)
    )
    token_positions = device_index * own_tokens + jnp.arange(own_tokens, dtype=jnp.int32)
    angles = token_positions.astype(F32)[:, None] * frequency[None, :]
    cosine = jnp.tile(jnp.cos(angles), (1, 4))
    sine_part = jnp.sin(angles)
    sine_part = jnp.concatenate([-sine_part, sine_part, -sine_part, sine_part], axis=1)

    def onward(block, across):
        route = []
        for i in range(group_size):
            goal = (i + (2 if i % 2 else -2)) % group_size
            route.append((i, goal ^ 1 if across else goal))
        return lax.ppermute(block.astype(jnp.float16), "expert", route).astype(F32)

    from_same = onward(same_far, False)
    from_cross = onward(cross_third, False)
    from_same = onward(same_third + from_same, False)
    from_same = onward(same_near[2] + from_same, False)
    from_cross = onward(cross_near[2] + from_cross, False)
    from_same = onward(same_near[1] + from_same, False)
    from_cross = onward(cross_near[1] + from_cross, True)
    mixture = (own + from_same + from_cross) * (1.0 / RETURN_SCALE)

    block_out, normed, own_kv = mix(
        packed, mixture, attn_gain[None], key_matrix, value_matrix, cosine, sine_part
    )
    ahead = [(i, i + 1) for i in range(group_size - 1)]
    halo_kv = lax.ppermute(own_kv, "expert", ahead)
    query = queries(normed, query_weight, cosine, sine_part)
    attended = attend(device_index.reshape(1), sinks, query, own_kv, halo_kv)
    return (block_out.T, attended)


def solution(mesh):
    in_specs = (
        P(("dp", "expert"), None),
        P(("dp", "expert"), None),
        P(("dp", "expert"), None),
        P("expert", None, None),
        P("expert", None, None),
        P("expert", None),
        P("expert", None, None),
        P("expert", None, None),
        P("expert", None),
        P(),
        P(),
        P(),
        P(),
        P(),
    )
    out_specs = (P(("dp", "expert"), None), P(("dp", "expert"), None))
    return jax.shard_map(body, mesh=mesh, in_specs=in_specs, out_specs=out_specs, check_vma=False)
```
